32 devices in a mesh: ew: 4 (over z), ns: 8 (over y, x, core).
Axes of the slice: x: 2, y: 2, z: 4, core: 2. Of those that a mesh axis runs over, the one named last changes fastest.
Arguments:
- tokens: bfloat16 [64, 128, 768], P('ns', 'ew'), may hold values from -16 to 16
- w_qkv: bfloat16 [768, 1152], replicated, may hold values from -0.21875 to 0.21875
- grad_out: bfloat16 [64, 128, 384], P('ns', 'ew'), may hold values from -6 to 6
Outputs:
- grad_tokens: bfloat16 [64, 128, 768], P('ns', 'ew')
- grad_w: bfloat16 [768, 1152], replicated
The draws below stay inside these ranges and needn't reach their ends.
All inputs are finite; a program needn't handle non-finite values.
Results may differ from the reference program's by a relative error of at most 0.005.
The reference program's roundings to bfloat16 on the way count: a program that leaves them out, or rounds other values in their place, can miss the bound.
Values may be sent and summed in bfloat16 or wider, within the bound.
A program may use at most 64 MiB of HBM per device.

```python
import jax
import jax.numpy as jnp
from jax import lax

D = 768
HEADS = 6
HDIM = 64
RADIUS = 6
RT = 8
CT = 32
ROWS = 64
COLS = 128


def draw_tokens(key, part):
    first_key = jax.random.fold_in(jax.random.fold_in(key, 11), 0)
    base = jax.random.normal(first_key, (ROWS, COLS, D), jnp.float32)
    values = jnp.clip(base, -4.0, 4.0)
    return values.astype(jnp.bfloat16)


def steps_of(key, shape, pieces, low, top_value):
    factor_of, own = 1.0, jax.random.fold_in(key, 6)
    for position, shards_of in pieces:
        heights = jnp.exp(jax.random.uniform(jax.random.fold_in(own, position), (shards_of,), jnp.float32, low / len(pieces), top_value / len(pieces)))
        factor_of = factor_of * jnp.repeat(heights, shape[position] // shards_of).reshape([-1 if axis == position else 1 for axis in range(len(shape))])
    return factor_of


def centred(key, dims, deviation, limit, shards=(), kind=jnp.bfloat16):
    array = jax.random.normal(key, dims, jnp.float32) * deviation
    if len(shards) > 0:
        array = steps_of(key, dims, shards, -0.22, 0.18) * array
    return jnp.clip(array, min=-limit, max=limit).astype(kind)


def setup_inputs(seed: int = 0) -> dict:
    arg_keys = jax.random.split(jax.random.key(seed), 4)
    tokens = draw_tokens(jax.random.fold_in(arg_keys[3], 71), 0)
    w_qkv = centred(arg_keys[1], (D, 3 * HEADS * HDIM), D ** -0.5, 0.21875)
    grad_out = centred(arg_keys[2], (ROWS, COLS, HEADS * HDIM), 1.0, 6.0, ((0, 8), (1, 4)))
    return dict(tokens=tokens, w_qkv=w_qkv, grad_out=grad_out)


def build_mask(row_start, col_start, tile_rows, tile_cols, grid_rows, grid_cols):
    query_rows = jnp.arange(tile_rows, dtype=jnp.int32)
    key_rows = jnp.arange(tile_rows + 2 * RADIUS, dtype=jnp.int32)
    global_rows = row_start - RADIUS + key_rows
    row_ok = (jnp.abs(query_rows[:, None] + RADIUS - key_rows[None, :]) <= RADIUS) & (global_rows >= 0)[None, :] & (global_rows < grid_rows)[None, :]
    query_cols = jnp.arange(tile_cols, dtype=jnp.int32)
    key_cols = jnp.arange(tile_cols + 2 * RADIUS, dtype=jnp.int32)
    global_cols = col_start - RADIUS + key_cols
    col_ok = (jnp.abs(query_cols[:, None] + RADIUS - key_cols[None, :]) <= RADIUS) & (global_cols >= 0)[None, :] & (global_cols < grid_cols)[None, :]
    both = row_ok[:, None, :, None] & col_ok[None, :, None, :]
    return both.reshape(tile_rows * tile_cols, (tile_rows + 2 * RADIUS) * (tile_cols + 2 * RADIUS))


def reference(tokens, w_qkv, grad_out):
    width = HEADS * HDIM
    scaling = HDIM ** -0.5
    qkv = jnp.dot(tokens.reshape(-1, D), w_qkv, preferred_element_type=jnp.float32).astype(jnp.bfloat16).reshape(ROWS, COLS, 3 * width)
    queries = qkv[:, :, :width]
    padded = jnp.pad(qkv[:, :, width:], ((RADIUS, RADIUS), (RADIUS, RADIUS), (0, 0)))
    tiles_down = ROWS // RT
    tiles_across = COLS // CT
    ext_rows = RT + 2 * RADIUS
    ext_cols = CT + 2 * RADIUS
    count = RT * CT

    def one_tile(totals, tile_index):
        row_start = (tile_index // tiles_across) * RT
        col_start = (tile_index % tiles_across) * CT
        zero = jnp.zeros((), jnp.int32)
        query_tile = lax.dynamic_slice(queries, (row_start, col_start, zero), (RT, CT, width)).reshape(count, HEADS, HDIM).astype(jnp.float32)
        extended = lax.dynamic_slice(padded, (row_start, col_start, zero), (ext_rows, ext_cols, 2 * width)).reshape(ext_rows * ext_cols, 2, HEADS, HDIM).astype(jnp.float32)
        key_tile = extended[:, 0]
        value_tile = extended[:, 1]
        cotangent = lax.dynamic_slice(grad_out, (row_start, col_start, zero), (RT, CT, width)).reshape(count, HEADS, HDIM).astype(jnp.float32)
        window = build_mask(row_start, col_start, RT, CT, ROWS, COLS)
        scores = jnp.einsum('qhd,khd->hqk', query_tile, key_tile) * scaling
        scores = jnp.where(window[None], scores, -1e30)
        row_max = jnp.max(scores, axis=-1, keepdims=True)
        exp_scores = jnp.exp(scores - row_max)
        probs = exp_scores / jnp.sum(exp_scores, axis=-1, keepdims=True)
        probs_low = lax.optimization_barrier(probs.astype(jnp.bfloat16)).astype(jnp.float32)
        attended = jnp.einsum('hqk,khd->qhd', probs_low, value_tile)
        delta_row = jnp.transpose(jnp.sum(cotangent * attended, axis=-1))[:, :, None]
        prob_grad = jnp.einsum('qhd,khd->hqk', cotangent, value_tile)
        score_grad = lax.optimization_barrier((probs * (prob_grad - delta_row)).astype(jnp.bfloat16)).astype(jnp.float32)
        query_grad = jnp.einsum('hqk,khd->qhd', score_grad, key_tile) * scaling
        key_grad = jnp.einsum('hqk,qhd->khd', score_grad, query_tile) * scaling
        value_grad = jnp.einsum('hqk,qhd->khd', probs_low, cotangent)
        tile_grads = jnp.stack([key_grad, value_grad], axis=1).reshape(ext_rows, ext_cols, 2 * width)
        current = lax.dynamic_slice(totals, (row_start, col_start, zero), (ext_rows, ext_cols, 2 * width))
        totals = lax.dynamic_update_slice(totals, current + tile_grads, (row_start, col_start, zero))
        return totals, query_grad.reshape(count, width)

    start = jnp.zeros((ROWS + 2 * RADIUS, COLS + 2 * RADIUS, 2 * width), jnp.float32)
    totals, query_grads = lax.scan(one_tile, start, jnp.arange(tiles_down * tiles_across, dtype=jnp.int32))
    kv_grads = totals[RADIUS:RADIUS + ROWS, RADIUS:RADIUS + COLS]
    query_grads = query_grads.reshape(tiles_down, tiles_across, RT, CT, width).transpose(0, 2, 1, 3, 4).reshape(ROWS, COLS, width)
    dqkv = jnp.concatenate([query_grads, kv_grads], axis=-1).astype(jnp.bfloat16).reshape(-1, 3 * width)
    grad_tokens = jnp.dot(dqkv, w_qkv.T, preferred_element_type=jnp.float32).astype(jnp.bfloat16).reshape(ROWS, COLS, D)
    grad_w = jnp.dot(tokens.reshape(-1, D).T, dqkv, preferred_element_type=jnp.float32).astype(jnp.bfloat16)
    return grad_tokens, grad_w
```

```python
import functools

import jax
import jax.numpy as jnp
from jax import lax
from jax.experimental import pallas as pl
from jax.experimental.pallas import tpu as pltpu
from jax.sharding import PartitionSpec as P

HEADS = 6
HDIM = 64
RADIUS = 6
MESH = pl.DeviceIdType.MESH


def padded(value, sides, width):
    for axis, dim in sides:
        size, length = (lax.axis_size(axis), value.shape[dim])
        up = [(i, (i + 1) % size) for i in range(size - 1)]
        down = [(j, i) for i, j in up]
        last = lax.slice_in_dim(value, length - width, length, axis=dim)
        leading = lax.slice_in_dim(value, 0, width, axis=dim)
        before = lax.ppermute(last, axis, up)
        after = lax.ppermute(leading, axis, down)
        value = jnp.concatenate([before, value, after], axis=dim)
    return value


def attention_kernel(nb, qr, qc, kr, kc, q_ref, k_ref, v_ref, g_ref, dq_ref, dk_ref, dv_ref):
    count = q_ref.shape[0] // nb
    span = kr.shape[2]
    step = (k_ref.shape[0] - span) // max(nb - 1, 1)
    dk_ref[...] = jnp.zeros_like(dk_ref)
    dv_ref[...] = jnp.zeros_like(dv_ref)
    for b in range(nb):
        rows = pl.ds(b * count, count)
        keys = pl.ds(b * step, span)
        ok = (jnp.abs(qr[rows, :] - kr[b]) <= RADIUS) & (jnp.abs(qc[rows, :] - kc[b]) <= RADIUS)
        bias = jnp.where(ok, 0.0, -1e30)
        q8 = q_ref[rows, :] * jnp.bfloat16(HDIM ** -0.5)
        kb, vb, g = k_ref[keys, :], v_ref[keys, :], g_ref[rows, :]
        dqs, dks, dvs = [], [], []
        for h in range(2):
            cols = slice(h * HDIM, (h + 1) * HDIM)
            qh, kh, vh, gh = q8[:, cols], kb[:, cols], vb[:, cols], g[:, cols]
            nt = (((1,), (1,)), ((), ()))
            tn = (((0,), (0,)), ((), ()))
            dot = functools.partial(lax.dot_general, preferred_element_type=jnp.float32)
            s = dot(qh, kh, nt) + bias
            e = jnp.exp(s - jnp.max(s, axis=1, keepdims=True))
            p = e * (1.0 / jnp.sum(e, axis=1, keepdims=True))
            pb = p.astype(jnp.bfloat16)
            att = jnp.dot(pb, vh, preferred_element_type=jnp.float32)
            delta = jnp.sum(gh.astype(jnp.float32) * att, axis=1, keepdims=True)
            dp = dot(gh, vh, nt)
            ds = (p * (dp - delta)).astype(jnp.bfloat16)
            dqs.append(jnp.dot(ds, kh, preferred_element_type=jnp.float32) * (HDIM ** -0.5))
            dks.append(dot(ds, qh, tn))
            dvs.append(dot(pb, gh, tn))
        dq_ref[rows, :] = jnp.concatenate(dqs, axis=1)
        dk_ref[keys, :] += jnp.concatenate(dks, axis=1)
        dv_ref[keys, :] += jnp.concatenate(dvs, axis=1)


def attention(q, kv, g, qr, qc, kr, kc, nb):
    count, width = q.shape
    extent = kv.shape[0]
    lanes = 2 * HDIM
    groups = width // lanes
    whole = lambda a: pl.BlockSpec(a.shape, lambda i: (0,) * a.ndim)
    qs = pl.BlockSpec((count, lanes), lambda i: (0, i))
    ks = pl.BlockSpec((extent, lanes), lambda i: (0, i))
    vs = pl.BlockSpec((extent, lanes), lambda i: (0, i + groups))
    return pl.pallas_call(
        functools.partial(attention_kernel, nb),
        grid=(groups,),
        in_specs=[whole(qr), whole(qc), whole(kr), whole(kc), qs, ks, vs, qs],
        out_specs=[qs, ks, ks],
        out_shape=[
            jax.ShapeDtypeStruct((count, width), jnp.float32),
            jax.ShapeDtypeStruct((extent, width), jnp.float32),
            jax.ShapeDtypeStruct((extent, width), jnp.float32),
        ],
        compiler_params=pltpu.CompilerParams(vmem_limit_bytes=40 << 20),
        cost_estimate=pl.CostEstimate(
            flops=14 * count * extent * width, bytes_accessed=8 << 20, transcendentals=count * extent * HEADS
        ),
    )(qr, qc, kr, kc, q, kv, kv, g)


CH = 128


def weight_kernel(
    nn, ne, tok_ref, dq_ref, out_ref, recv, part, slots,
    a_send, a_recv, r_send, r_recv, z_send, z_recv, p_send, p_recv, f_send, f_recv,
):
    e, n = lax.axis_index("ew"), lax.axis_index("ns")
    share = recv.shape[1]
    count = tok_ref.shape[0] // nn
    chunks = part.shape[0]
    owner = [min((c + 1) // 2, ne - 1) for c in range(chunks)]
    slot_of = [sum(1 for d in range(c) if owner[d] == owner[c]) for c in range(chunks)]
    core = lax.rem(n, 2)
    sibling = n + 1 - 2 * core

    def rows_of(d):
        return pl.ds(pl.multiple_of(d * share, 16), share)

    def at(d, m):
        return (d, m)

    barrier = pltpu.get_barrier_semaphore()
    for k in range(1, nn):
        pl.semaphore_signal(barrier, inc=1, device_id=at(e, lax.rem(n + k, nn)), device_id_type=MESH)
    for k in range(1, ne):
        pl.semaphore_signal(barrier, inc=1, device_id=at(lax.rem(e + k, ne), n), device_id_type=MESH)
    pl.semaphore_wait(barrier, nn - 1 + ne - 1)

    def exchange(k):
        to = lax.rem(n + k, nn)
        return pltpu.make_async_remote_copy(
            src_ref=dq_ref.at[rows_of(to)], dst_ref=recv.at[n],
            send_sem=a_send.at[k], recv_sem=a_recv.at[n],
            device_id=at(e, to), device_id_type=MESH,
        )

    def arrived(k):
        src = lax.rem(n + nn - k, nn)
        return pltpu.make_async_remote_copy(
            src_ref=recv.at[src], dst_ref=recv.at[src],
            send_sem=a_send.at[k], recv_sem=a_recv.at[src],
            device_id=at(e, src), device_id_type=MESH,
        )

    for k in range(1, nn):
        exchange(k).start()
    recv[n] = dq_ref[rows_of(n), :]
    for k in range(1, nn):
        arrived(k).wait_recv()

    def reduce_copy(c, src):
        return pltpu.make_async_remote_copy(
            src_ref=part.at[c], dst_ref=slots.at[slot_of[c], src],
            send_sem=r_send.at[c], recv_sem=r_recv.at[slot_of[c], src],
            device_id=at(owner[c], n), device_id_type=MESH,
        )

    order = [c for c in range(chunks)]
    for c in order:
        total = jnp.zeros((share, CH), jnp.float32)
        for s in range(nn):
            total += jnp.dot(
                recv[s], tok_ref[s * count : (s + 1) * count, c * CH : (c + 1) * CH],
                preferred_element_type=jnp.float32,
            )
        part[c] = total

        @pl.when(e != owner[c])
        def _():
            reduce_copy(c, e).start()

    def spot(c, m):
        return out_ref.at[rows_of(m), c * CH : (c + 1) * CH]

    def column_copy(c, k):
        return pltpu.make_async_remote_copy(
            src_ref=spot(c, n), dst_ref=spot(c, n),
            send_sem=z_send.at[c, k], recv_sem=z_recv.at[c],
            device_id=at(lax.rem(owner[c] + k, ne), n), device_id_type=MESH,
        )

    def plane_copy(c, m, to, sem, k, rsem):
        return pltpu.make_async_remote_copy(
            src_ref=spot(c, m), dst_ref=spot(c, m),
            send_sem=sem.at[c, k], recv_sem=rsem.at[c, m],
            device_id=at(e, to), device_id_type=MESH,
        )

    def peers(k):
        return lax.rem(n + 2 * k, nn)

    def spread(c):
        for k in range(1, nn // 2):
            plane_copy(c, n, peers(k), p_send, k, p_recv).start()
        plane_copy(c, n, sibling, p_send, 0, p_recv).start()

    for c in order:

        @pl.when(e == owner[c])
        def _():
            total = part[c]
            for k in range(1, ne):
                src = (owner[c] + k) % ne
                reduce_copy(c, src).wait_recv()
                total += slots[slot_of[c], src]
            out_ref[rows_of(n), c * CH : (c + 1) * CH] = total.astype(jnp.bfloat16)
            for k in range(1, ne):
                column_copy(c, k).start()
            spread(c)

    for c in order:

        @pl.when(e != owner[c])
        def _():
            column_copy(c, 1).wait_recv()
            spread(c)

    for c in order:
        for k in range(1, nn // 2):
            m = peers(k)
            plane_copy(c, m, sibling, p_send, 0, p_recv).wait_recv()
            plane_copy(c, m, sibling, f_send, k, f_recv).start()

    for c in order:
        plane_copy(c, sibling, sibling, p_send, 0, p_recv).wait_recv()
        for k in range(1, nn // 2):
            m = lax.rem(sibling + 2 * k, nn)
            plane_copy(c, m, sibling, f_send, k, f_recv).wait_recv()

    for k in range(1, nn):
        exchange(k).wait_send()
    for c in order:

        @pl.when(e != owner[c])
        def _():
            reduce_copy(c, e).wait_send()

        @pl.when(e == owner[c])
        def _():
            for k in range(1, ne):
                column_copy(c, k).wait_send()

        for k in range(nn // 2):
            plane_copy(c, n, sibling, p_send, k, p_recv).wait_send()
        for k in range(1, nn // 2):
            plane_copy(c, n, sibling, f_send, k, f_recv).wait_send()


def weight_sum(tok_all, dqkv_t, nn, ne):
    wide, count = dqkv_t.shape
    features = tok_all.shape[1]
    share, chunks = wide // nn, features // CH
    dma = pltpu.SemaphoreType.DMA
    vm = pl.BlockSpec(memory_space=pltpu.VMEM)
    return pl.pallas_call(
        functools.partial(weight_kernel, nn, ne),
        out_shape=jax.ShapeDtypeStruct((wide, features), jnp.bfloat16),
        in_specs=[vm, vm],
        out_specs=vm,
        scratch_shapes=[
            pltpu.VMEM((nn, share, count), jnp.bfloat16),
            pltpu.VMEM((chunks, share, CH), jnp.float32),
            pltpu.VMEM((2, ne, share, CH), jnp.float32),
            dma((nn,)), dma((nn,)),
            dma((chunks,)), dma((2, ne)),
            dma((chunks, ne)), dma((chunks,)),
            dma((chunks, nn // 2)), dma((chunks, nn)),
            dma((chunks, nn // 2)), dma((chunks, nn)),
        ],
        compiler_params=pltpu.CompilerParams(
            collective_id=1, has_side_effects=True, vmem_limit_bytes=40 << 20
        ),
        cost_estimate=pl.CostEstimate(
            flops=2 * share * nn * count * features, bytes_accessed=8 << 20, transcendentals=0
        ),
    )(tok_all, dqkv_t)


def local(tokens, w_qkv, grad_out):
    tile_rows, tile_cols, features = tokens.shape
    nn, ne = lax.axis_size("ns"), lax.axis_size("ew")
    width = w_qkv.shape[1] // 3
    count = tile_rows * tile_cols
    flat_tokens = tokens.reshape(count, features)
    paired = nn == 8 and ne == 4
    if paired:
        tok_all = lax.all_gather(flat_tokens, "ns", axis=0, tiled=True)
    projected = jnp.dot(flat_tokens, w_qkv, preferred_element_type=jnp.float32).astype(jnp.bfloat16)
    wide_kv = padded(
        projected[:, width:].reshape(tile_rows, tile_cols, 2 * width),
        (("ew", 1), ("ns", 0)),
        RADIUS,
    )
    ext_rows, ext_cols = (wide_kv.shape[0], wide_kv.shape[1])
    key_values = wide_kv.reshape(ext_rows * ext_cols, 2 * width)
    nb = 2
    row0 = lax.axis_index("ns") * tile_rows
    col0 = lax.axis_index("ew") * tile_cols
    qi = jnp.arange(count, dtype=jnp.int32)
    qr = (row0 + qi // tile_cols)[:, None]
    qc = (col0 + qi % tile_cols)[:, None]
    ki = jnp.arange(ext_rows * ext_cols, dtype=jnp.int32)
    kr = row0 - RADIUS + ki // ext_cols
    kc = col0 - RADIUS + ki % ext_cols
    inside = (kr >= 0) & (kr < nn * tile_rows) & (kc >= 0) & (kc < ne * tile_cols)
    kr = jnp.where(inside, kr, -1000)
    per = tile_rows // nb
    span = (per + 2 * RADIUS) * ext_cols
    pick = lambda a: jnp.stack([a[b * per * ext_cols :][:span][None] for b in range(nb)])
    query_grad, key_grad, value_grad = attention(
        projected[:, :width], key_values, grad_out.reshape(count, width), qr, qc, pick(kr), pick(kc), nb
    )
    ext_grads = jnp.concatenate([key_grad, value_grad], axis=1).reshape(ext_rows, ext_cols, 2 * width)
    side_strips = jnp.concatenate([ext_grads[:, :RADIUS], ext_grads[:, tile_cols + RADIUS :]], axis=1)
    from_sides = padded(side_strips, (("ew", 1),), RADIUS)
    middle = ext_grads[:, RADIUS : tile_cols + RADIUS]
    middle = middle + jnp.pad(from_sides[:, :RADIUS], ((0, 0), (0, tile_cols - RADIUS), (0, 0)))
    middle = middle + jnp.pad(from_sides[:, 3 * RADIUS :], ((0, 0), (tile_cols - RADIUS, 0), (0, 0)))
    edge_strips = jnp.concatenate([middle[:RADIUS], middle[tile_rows + RADIUS :]], axis=0)
    from_edges = padded(edge_strips, (("ns", 0),), RADIUS)
    owned = middle[RADIUS : tile_rows + RADIUS]
    owned = owned + jnp.pad(from_edges[:RADIUS], ((0, tile_rows - RADIUS), (0, 0), (0, 0)))
    owned = owned + jnp.pad(from_edges[3 * RADIUS :], ((tile_rows - RADIUS, 0), (0, 0), (0, 0)))
    dqkv = jnp.concatenate([query_grad, owned.reshape(count, 2 * width)], axis=1).astype(
        jnp.bfloat16
    )
    grad_tokens = (
        jnp.dot(dqkv, w_qkv.T, preferred_element_type=jnp.float32)
        .astype(jnp.bfloat16)
        .reshape(tile_rows, tile_cols, features)
    )
    if paired:
        grad_w = weight_sum(tok_all, dqkv.T, nn, ne).T
    else:
        weight_part = lax.dot_general(
            flat_tokens, dqkv, (((0,), (0,)), ((), ())), preferred_element_type=jnp.float32
        )
        grad_w = lax.psum(weight_part, ("ew", "ns")).astype(jnp.bfloat16)
    return (grad_tokens, grad_w)


def solution(mesh):
    in_specs = (P("ns", "ew", None), P(), P("ns", "ew", None))
    out_specs = (P("ns", "ew", None), P())
    return jax.shard_map(local, mesh=mesh, in_specs=in_specs, out_specs=out_specs, check_vma=False)
```

```python
import functools

import jax
import jax.numpy as jnp
import numpy as np
from jax import lax
from jax.experimental import pallas as pl
from jax.experimental.pallas import tpu as pltpu
from jax.sharding import PartitionSpec as P

HEADS = 6
HDIM = 64
RADIUS = 6
MESH = pl.DeviceIdType.MESH


DIRS = [(dn, de) for dn in (-1, 0, 1) for de in (-1, 0, 1) if (dn, de) != (0, 0)]


def halo_attention_kernel(
    nn, ne, qr, qc, kr, kc, qkv_ref, first_ref, last_ref, g_ref, out_ref, ext, acc, *rest
):
    back = rest[:8]
    f_send, f_recv, b_send, b_recv = rest[8:]
    e, n = lax.axis_index("ew"), lax.axis_index("ns")
    pairs, wide, total = qkv_ref.shape
    width = total // 3
    half = RADIUS // 2
    groups, lanes = width // 128, 128
    slots = ext.shape[1]
    side = (slots - wide) // 2
    nb = kr.shape[0]
    step = pairs // nb
    tall = step + 2 * half
    cols = wide // 2

    def exists(d):
        dn, de = d
        return (n + dn >= 0) & (n + dn < nn) & (e + de >= 0) & (e + de < ne)

    def own_pairs(dn):
        return {-1: pl.ds(0, half), 0: pl.ds(0, pairs), 1: pl.ds(pairs - half, half)}[dn]

    def region(d):
        rows = {-1: pl.ds(0, half), 0: pl.ds(half, pairs), 1: pl.ds(half + pairs, half)}[d[0]]
        place = {0: pl.ds(0, wide), 1: pl.ds(wide, side), -1: pl.ds(wide + side, side)}[d[1]]
        return rows, place

    def opposite(i):
        return DIRS.index((-DIRS[i][0], -DIRS[i][1]))

    def forward(i):
        dn, de = DIRS[i]
        rows = own_pairs(dn)
        if de == 0:
            src = qkv_ref.at[rows, :, pl.ds(width, 2 * width)]
        else:
            src = (first_ref if de < 0 else last_ref).at[rows]
        there = opposite(i)
        a, b = region(DIRS[there])
        return pltpu.make_async_remote_copy(
            src_ref=src, dst_ref=ext.at[a, b], send_sem=f_send.at[i], recv_sem=f_recv.at[there],
            device_id=(e + de, n + dn), device_id_type=MESH,
        )

    def forward_in(i):
        a, b = region(DIRS[i])
        return pltpu.make_async_remote_copy(
            src_ref=ext.at[a, b], dst_ref=ext.at[a, b], send_sem=f_send.at[i], recv_sem=f_recv.at[i],
            device_id=(e + DIRS[i][1], n + DIRS[i][0]), device_id_type=MESH,
        )

    def backward(i, grp):
        a, b = region(DIRS[i])
        there = opposite(i)
        return pltpu.make_async_remote_copy(
            src_ref=acc.at[grp, a, b], dst_ref=back[there].at[grp],
            send_sem=b_send.at[i, grp], recv_sem=b_recv.at[there, grp],
            device_id=(e + DIRS[i][1], n + DIRS[i][0]), device_id_type=MESH,
        )

    def backward_in(i, grp):
        return pltpu.make_async_remote_copy(
            src_ref=back[i].at[grp], dst_ref=back[i].at[grp],
            send_sem=b_send.at[i, grp], recv_sem=b_recv.at[i, grp],
            device_id=(e + DIRS[i][1], n + DIRS[i][0]), device_id_type=MESH,
        )

    barrier = pltpu.get_barrier_semaphore()
    for d in DIRS:

        @pl.when(exists(d))
        def _():
            pl.semaphore_signal(barrier, inc=1, device_id=(e + d[1], n + d[0]), device_id_type=MESH)

    pl.semaphore_wait(barrier, sum(exists(d).astype(jnp.int32) for d in DIRS))

    for i, d in enumerate(DIRS):

        @pl.when(exists(d))
        def _():
            forward(i).start()

    ext[pl.ds(half, pairs), pl.ds(0, wide), :] = qkv_ref[:, :, pl.ds(width, 2 * width)]
    acc[...] = jnp.zeros_like(acc)
    for i, d in enumerate(DIRS):
        a, b = region(d)

        @pl.when(jnp.logical_not(exists(d)))
        def _():
            ext[a, b, :] = jnp.zeros((a.size, b.size, 2 * width), ext.dtype)

        @pl.when(exists(d))
        def _():
            forward_in(i).wait_recv()

    nt = (((1,), (1,)), ((), ()))
    tn = (((0,), (0,)), ((), ()))
    dot = functools.partial(lax.dot_general, preferred_element_type=jnp.float32)
    count = step * wide

    def one_group(grp, carry):
        at = pl.multiple_of(grp * lanes, lanes)
        at_v = pl.multiple_of(grp * lanes + width, lanes)
        for b in range(nb):
            rows = pl.ds(b * step, step)
            keys = pl.ds(b * step, tall)
            flat = pl.ds(b * count, count)
            ok = (jnp.abs(qr[flat, :] - kr[b]) <= RADIUS) & (jnp.abs(qc[flat, :] - kc[b]) <= RADIUS)
            bias = jnp.where(ok, 0.0, -1e30)
            q8 = qkv_ref[rows, :, pl.ds(at, lanes)].reshape(count, lanes) * jnp.bfloat16(HDIM ** -0.5)
            g = g_ref[rows, :, pl.ds(at, lanes)].reshape(count, lanes)
            kb = ext[keys, :, pl.ds(at, lanes)].reshape(tall * slots, lanes)
            vb = ext[keys, :, pl.ds(at_v, lanes)].reshape(tall * slots, lanes)
            dqs, dks, dvs = [], [], []
            for h in range(2):
                part = slice(h * HDIM, (h + 1) * HDIM)
                qh, kh, vh, gh = q8[:, part], kb[:, part], vb[:, part], g[:, part]
                s = dot(qh, kh, nt) + bias
                ex = jnp.exp(s - jnp.max(s, axis=1, keepdims=True))
                p = ex * (1.0 / jnp.sum(ex, axis=1, keepdims=True))
                pb = p.astype(jnp.bfloat16)
                att = jnp.dot(pb, vh, preferred_element_type=jnp.float32)
                delta = jnp.sum(gh.astype(jnp.float32) * att, axis=1, keepdims=True)
                dp = dot(gh, vh, nt)
                ds = (p * (dp - delta)).astype(jnp.bfloat16)
                dqs.append(jnp.dot(ds, kh, preferred_element_type=jnp.float32) * (HDIM ** -0.5))
                dks.append(dot(ds, qh, tn))
                dvs.append(dot(pb, gh, tn))
            dq = jnp.concatenate(dqs, axis=1).astype(out_ref.dtype)
            out_ref[rows, :, pl.ds(at, lanes)] = dq.reshape(step, wide, lanes)
            both = jnp.concatenate(dks + dvs, axis=1).reshape(tall, slots, 2 * lanes)
            acc[grp, keys] += both
        for i, d in enumerate(DIRS):

            @pl.when(exists(d))
            def _():
                backward(i, grp).start()

        return carry

    lax.fori_loop(0, groups, one_group, 0)

    def collect(grp, carry):
        for i, d in enumerate(DIRS):
            mine = own_pairs(d[0])
            here = pl.ds(half + mine.start, mine.size)

            @pl.when(exists(d))
            def _():
                backward_in(i, grp).wait_recv()
                if d[1] == 0:
                    acc[grp, here, pl.ds(0, wide)] += back[i][grp]
                else:
                    for r in range(2):
                        to = r * cols + (0 if d[1] < 0 else cols - side // 2)
                        acc[grp, here, pl.ds(to, side // 2)] += back[i][grp, :, pl.ds(r * side // 2, side // 2)]

        for j in range(2):
            to = pl.multiple_of(grp * lanes + (j + 1) * width, lanes)
            own = acc[grp, pl.ds(half, pairs), pl.ds(0, wide), pl.ds(j * lanes, lanes)]
            out_ref[:, :, pl.ds(to, lanes)] = own.astype(out_ref.dtype)
        return carry

    lax.fori_loop(0, groups, collect, 0)

    for i, d in enumerate(DIRS):

        @pl.when(exists(d))
        def _():
            forward(i).wait_send()
            for grp in range(groups):
                backward(i, grp).wait_send()


def halo_attention(qkv, first, last, g, qr, qc, kr, kc, slots, nn, ne):
    pairs, wide, total = qkv.shape
    half, width = RADIUS // 2, total // 3
    groups, side = width // 128, (slots - wide) // 2
    tall = pairs + 2 * half
    dma = pltpu.SemaphoreType.DMA
    vm = pl.BlockSpec(memory_space=pltpu.VMEM)
    back = [
        pltpu.VMEM((groups, half if dn else pairs, side if de else wide, 256), jnp.float32)
        for dn, de in DIRS
    ]
    return pl.pallas_call(
        functools.partial(halo_attention_kernel, nn, ne),
        out_shape=jax.ShapeDtypeStruct(qkv.shape, jnp.bfloat16),
        in_specs=[vm] * 8,
        out_specs=vm,
        scratch_shapes=[
            pltpu.VMEM((tall, slots, 2 * width), jnp.bfloat16),
            pltpu.VMEM((groups, tall, slots, 256), jnp.float32),
        ]
        + back
        + [dma((8,)), dma((8,)), dma((8, groups)), dma((8, groups))],
        compiler_params=pltpu.CompilerParams(
            collective_id=2, has_side_effects=True, vmem_limit_bytes=44 << 20
        ),
        cost_estimate=pl.CostEstimate(
            flops=14 * pairs * wide * tall * slots * width,
            bytes_accessed=4 << 20,
            transcendentals=pairs * wide * tall * slots * HEADS,
        ),
    )(qr, qc, kr, kc, qkv, first, last, g)


CH = 128


def weight_kernel(
    nn, ne, tok_ref, dq_ref, out_ref, recv, part, slots,
    a_send, a_recv, r_send, r_recv, z_send, z_recv, p_send, p_recv, f_send, f_recv,
):
    e, n = lax.axis_index("ew"), lax.axis_index("ns")
    share = recv.shape[1]
    count = tok_ref.shape[0] // nn
    chunks = part.shape[0]
    owner = [min((c + 1) // 2, ne - 1) for c in range(chunks)]
    slot_of = [sum(1 for d in range(c) if owner[d] == owner[c]) for c in range(chunks)]
    core = lax.rem(n, 2)
    sibling = n + 1 - 2 * core

    def rows_of(d):
        return pl.ds(pl.multiple_of(d * share, 16), share)

    def at(d, m):
        return (d, m)

    barrier = pltpu.get_barrier_semaphore()
    for k in range(1, nn):
        pl.semaphore_signal(barrier, inc=1, device_id=at(e, lax.rem(n + k, nn)), device_id_type=MESH)
    for k in range(1, ne):
        pl.semaphore_signal(barrier, inc=1, device_id=at(lax.rem(e + k, ne), n), device_id_type=MESH)
    pl.semaphore_wait(barrier, nn - 1 + ne - 1)

    def exchange(k):
        to = lax.rem(n + k, nn)
        return pltpu.make_async_remote_copy(
            src_ref=dq_ref.at[rows_of(to)], dst_ref=recv.at[n],
            send_sem=a_send.at[k], recv_sem=a_recv.at[n],
            device_id=at(e, to), device_id_type=MESH,
        )

    def arrived(k):
        src = lax.rem(n + nn - k, nn)
        return pltpu.make_async_remote_copy(
            src_ref=recv.at[src], dst_ref=recv.at[src],
            send_sem=a_send.at[k], recv_sem=a_recv.at[src],
            device_id=at(e, src), device_id_type=MESH,
        )

    for k in range(1, nn):
        exchange(k).start()
    recv[n] = dq_ref[rows_of(n), :]
    for k in range(1, nn):
        arrived(k).wait_recv()

    def reduce_copy(c, src):
        return pltpu.make_async_remote_copy(
            src_ref=part.at[c], dst_ref=slots.at[slot_of[c], src],
            send_sem=r_send.at[c], recv_sem=r_recv.at[slot_of[c], src],
            device_id=at(owner[c], n), device_id_type=MESH,
        )

    order = [c for c in range(chunks)]
    for c in order:
        total = jnp.zeros((share, CH), jnp.float32)
        for s in range(nn):
            total += jnp.dot(
                recv[s], tok_ref[s * count : (s + 1) * count, c * CH : (c + 1) * CH],
                preferred_element_type=jnp.float32,
            )
        part[c] = total

        @pl.when(e != owner[c])
        def _():
            reduce_copy(c, e).start()

    def spot(c, m):
        return out_ref.at[rows_of(m), c * CH : (c + 1) * CH]

    def column_copy(c, k):
        return pltpu.make_async_remote_copy(
            src_ref=spot(c, n), dst_ref=spot(c, n),
            send_sem=z_send.at[c, k], recv_sem=z_recv.at[c],
            device_id=at(lax.rem(owner[c] + k, ne), n), device_id_type=MESH,
        )

    def plane_copy(c, m, to, sem, k, rsem):
        return pltpu.make_async_remote_copy(
            src_ref=spot(c, m), dst_ref=spot(c, m),
            send_sem=sem.at[c, k], recv_sem=rsem.at[c, m],
            device_id=at(e, to), device_id_type=MESH,
        )

    def peers(k):
        return lax.rem(n + 2 * k, nn)

    def spread(c):
        for k in range(1, nn // 2):
            plane_copy(c, n, peers(k), p_send, k, p_recv).start()
        plane_copy(c, n, sibling, p_send, 0, p_recv).start()

    for c in order:

        @pl.when(e == owner[c])
        def _():
            total = part[c]
            for k in range(1, ne):
                src = (owner[c] + k) % ne
                reduce_copy(c, src).wait_recv()
                total += slots[slot_of[c], src]
            out_ref[rows_of(n), c * CH : (c + 1) * CH] = total.astype(jnp.bfloat16)
            for k in range(1, ne):
                column_copy(c, k).start()
            spread(c)

    for c in order:

        @pl.when(e != owner[c])
        def _():
            column_copy(c, 1).wait_recv()
            spread(c)

    for c in order:
        for k in range(1, nn // 2):
            m = peers(k)
            plane_copy(c, m, sibling, p_send, 0, p_recv).wait_recv()
            plane_copy(c, m, sibling, f_send, k, f_recv).start()

    for c in order:
        plane_copy(c, sibling, sibling, p_send, 0, p_recv).wait_recv()
        for k in range(1, nn // 2):
            m = lax.rem(sibling + 2 * k, nn)
            plane_copy(c, m, sibling, f_send, k, f_recv).wait_recv()

    for k in range(1, nn):
        exchange(k).wait_send()
    for c in order:

        @pl.when(e != owner[c])
        def _():
            reduce_copy(c, e).wait_send()

        @pl.when(e == owner[c])
        def _():
            for k in range(1, ne):
                column_copy(c, k).wait_send()

        for k in range(nn // 2):
            plane_copy(c, n, sibling, p_send, k, p_recv).wait_send()
        for k in range(1, nn // 2):
            plane_copy(c, n, sibling, f_send, k, f_recv).wait_send()


def weight_sum(tok_all, dqkv_t, nn, ne):
    wide, count = dqkv_t.shape
    features = tok_all.shape[1]
    share, chunks = wide // nn, features // CH
    dma = pltpu.SemaphoreType.DMA
    vm = pl.BlockSpec(memory_space=pltpu.VMEM)
    return pl.pallas_call(
        functools.partial(weight_kernel, nn, ne),
        out_shape=jax.ShapeDtypeStruct((wide, features), jnp.bfloat16),
        in_specs=[vm, vm],
        out_specs=vm,
        scratch_shapes=[
            pltpu.VMEM((nn, share, count), jnp.bfloat16),
            pltpu.VMEM((chunks, share, CH), jnp.float32),
            pltpu.VMEM((2, ne, share, CH), jnp.float32),
            dma((nn,)), dma((nn,)),
            dma((chunks,)), dma((2, ne)),
            dma((chunks, ne)), dma((chunks,)),
            dma((chunks, nn // 2)), dma((chunks, nn)),
            dma((chunks, nn // 2)), dma((chunks, nn)),
        ],
        compiler_params=pltpu.CompilerParams(
            collective_id=1, has_side_effects=True, vmem_limit_bytes=40 << 20
        ),
        cost_estimate=pl.CostEstimate(
            flops=2 * share * nn * count * features, bytes_accessed=8 << 20, transcendentals=0
        ),
    )(tok_all, dqkv_t)


def local(tokens, w_qkv, grad_out):
    tile_rows, tile_cols, features = tokens.shape
    nn, ne = lax.axis_size("ns"), lax.axis_size("ew")
    width = w_qkv.shape[1] // 3
    count = tile_rows * tile_cols
    flat_tokens = tokens.reshape(count, features)
    paired = nn == 8 and ne == 4
    if paired:
        tok_all = lax.all_gather(flat_tokens, "ns", axis=0, tiled=True)
    projected = jnp.dot(flat_tokens, w_qkv, preferred_element_type=jnp.float32).astype(jnp.bfloat16)
    half, pairs, wide, edge = RADIUS // 2, tile_rows // 2, 2 * tile_cols, 8
    slots = wide + 4 * edge
    qkv = projected.reshape(pairs, wide, 3 * width)
    by_row = projected[:, width:].reshape(tile_rows, tile_cols, 2 * width)
    first = by_row[:, :edge].reshape(pairs, 2 * edge, 2 * width)
    last = by_row[:, tile_cols - edge :].reshape(pairs, 2 * edge, 2 * width)
    nb = 2
    row0 = lax.axis_index("ns") * tile_rows
    col0 = lax.axis_index("ew") * tile_cols
    qi = jnp.arange(count, dtype=jnp.int32)
    qr = (row0 + qi // tile_cols)[:, None]
    qc = (col0 + qi % tile_cols)[:, None]
    slot = np.arange(slots)
    in_side = np.maximum(slot - wide, 0)
    slot_row = np.where(slot < wide, slot // tile_cols, (in_side % (2 * edge)) // edge)
    slot_col = np.where(
        slot < wide,
        slot % tile_cols,
        np.where(in_side < 2 * edge, tile_cols + in_side % edge, in_side % edge - edge),
    )
    ext_row = (2 * np.arange(pairs + 2 * half)[:, None] - RADIUS + slot_row[None]).astype(np.int32)
    ext_col = np.broadcast_to(slot_col[None], ext_row.shape).astype(np.int32)
    kr, kc = row0 + ext_row, col0 + ext_col
    inside = (kr >= 0) & (kr < nn * tile_rows) & (kc >= 0) & (kc < ne * tile_cols)
    kr = jnp.where(inside, kr, -1000)
    per = pairs // nb
    pick = lambda a: jnp.stack([a[b * per : b * per + per + 2 * half].reshape(1, -1) for b in range(nb)])
    dqkv = halo_attention(
        qkv, first, last, grad_out.reshape(pairs, wide, width), qr, qc, pick(kr), pick(kc), slots, nn, ne
    ).reshape(count, 3 * width)
    grad_tokens = (
        jnp.dot(dqkv, w_qkv.T, preferred_element_type=jnp.float32)
        .astype(jnp.bfloat16)
        .reshape(tile_rows, tile_cols, features)
    )
    if paired:
        grad_w = weight_sum(tok_all, dqkv.T, nn, ne).T
    else:
        weight_part = lax.dot_general(
            flat_tokens, dqkv, (((0,), (0,)), ((), ())), preferred_element_type=jnp.float32
        )
        grad_w = lax.psum(weight_part, ("ew", "ns")).astype(jnp.bfloat16)
    return (grad_tokens, grad_w)


def solution(mesh):
    in_specs = (P("ns", "ew", None), P(), P("ns", "ew", None))
    out_specs = (P("ns", "ew", None), P())
    return jax.shard_map(local, mesh=mesh, in_specs=in_specs, out_specs=out_specs, check_vma=False)
```

```python
import functools

import jax
import jax.numpy as jnp
import numpy as np
from jax import lax
from jax.experimental import pallas as pl
from jax.experimental.pallas import tpu as pltpu
from jax.sharding import PartitionSpec as P

HEADS = 6
HDIM = 64
RADIUS = 6
MESH = pl.DeviceIdType.MESH


DIRS = [(dn, de) for dn in (-1, 0, 1) for de in (-1, 0, 1) if (dn, de) != (0, 0)]


def halo_attention_kernel(
    nn, ne, more, qr, qc, kr, kc, qkv_ref, first_ref, last_ref, g_ref, out_ref, ext, acc, *rest
):
    back = rest[:8]
    f_send, f_recv, b_send, b_recv = rest[8:]
    e, n = lax.axis_index("ew"), lax.axis_index("ns")
    pairs, wide, total = qkv_ref.shape
    width = total // 3
    half = RADIUS // 2
    groups, lanes = width // 128, 128
    slots = ext.shape[1]
    side = (slots - wide) // 2
    nb = kr.shape[0]
    step = pairs // nb
    tall = step + 2 * half
    cols = wide // 2

    def exists(d):
        dn, de = d
        return (n + dn >= 0) & (n + dn < nn) & (e + de >= 0) & (e + de < ne)

    def own_pairs(dn):
        return {-1: pl.ds(0, half), 0: pl.ds(0, pairs), 1: pl.ds(pairs - half, half)}[dn]

    def region(d):
        rows = {-1: pl.ds(0, half), 0: pl.ds(half, pairs), 1: pl.ds(half + pairs, half)}[d[0]]
        place = {0: pl.ds(0, wide), 1: pl.ds(wide, side), -1: pl.ds(wide + side, side)}[d[1]]
        return rows, place

    def opposite(i):
        return DIRS.index((-DIRS[i][0], -DIRS[i][1]))

    def forward(i):
        dn, de = DIRS[i]
        rows = own_pairs(dn)
        if de == 0:
            src = qkv_ref.at[rows, :, pl.ds(width, 2 * width)]
        else:
            src = (first_ref if de < 0 else last_ref).at[rows]
        there = opposite(i)
        a, b = region(DIRS[there])
        return pltpu.make_async_remote_copy(
            src_ref=src, dst_ref=ext.at[a, b], send_sem=f_send.at[i], recv_sem=f_recv.at[there],
            device_id=(e + de, n + dn), device_id_type=MESH,
        )

    def forward_in(i):
        a, b = region(DIRS[i])
        return pltpu.make_async_remote_copy(
            src_ref=ext.at[a, b], dst_ref=ext.at[a, b], send_sem=f_send.at[i], recv_sem=f_recv.at[i],
            device_id=(e + DIRS[i][1], n + DIRS[i][0]), device_id_type=MESH,
        )

    def backward(i, grp):
        a, b = region(DIRS[i])
        there = opposite(i)
        return pltpu.make_async_remote_copy(
            src_ref=acc.at[grp, a, b], dst_ref=back[there].at[grp],
            send_sem=b_send.at[i, grp], recv_sem=b_recv.at[there, grp],
            device_id=(e + DIRS[i][1], n + DIRS[i][0]), device_id_type=MESH,
        )

    def backward_in(i, grp):
        return pltpu.make_async_remote_copy(
            src_ref=back[i].at[grp], dst_ref=back[i].at[grp],
            send_sem=b_send.at[i, grp], recv_sem=b_recv.at[i, grp],
            device_id=(e + DIRS[i][1], n + DIRS[i][0]), device_id_type=MESH,
        )

    near = DIRS
    barrier = pltpu.get_barrier_semaphore()
    if more is not None:
        near = [d for d in DIRS if d[0] and d[1]]
        for k in range(1, nn):
            pl.semaphore_signal(barrier, inc=1, device_id=(e, lax.rem(n + k, nn)), device_id_type=MESH)
        for k in range(1, ne):
            pl.semaphore_signal(barrier, inc=1, device_id=(lax.rem(e + k, ne), n), device_id_type=MESH)
    for d in near:

        @pl.when(exists(d))
        def _():
            pl.semaphore_signal(barrier, inc=1, device_id=(e + d[1], n + d[0]), device_id_type=MESH)

    others = nn - 1 + ne - 1 if more is not None else 0
    pl.semaphore_wait(barrier, others + sum(exists(d).astype(jnp.int32) for d in near))

    for i, d in enumerate(DIRS):

        @pl.when(exists(d))
        def _():
            forward(i).start()

    ext[pl.ds(half, pairs), pl.ds(0, wide), :] = qkv_ref[:, :, pl.ds(width, 2 * width)]
    acc[...] = jnp.zeros_like(acc)
    for i, d in enumerate(DIRS):
        a, b = region(d)

        @pl.when(jnp.logical_not(exists(d)))
        def _():
            ext[a, b, :] = jnp.zeros((a.size, b.size, 2 * width), ext.dtype)

        @pl.when(exists(d))
        def _():
            forward_in(i).wait_recv()

    if more is not None:
        more.start()
    nt = (((1,), (1,)), ((), ()))
    tn = (((0,), (0,)), ((), ()))
    dot = functools.partial(lax.dot_general, preferred_element_type=jnp.float32)
    count = step * wide

    def one_group(grp, carry):
        at = pl.multiple_of(grp * lanes, lanes)
        at_v = pl.multiple_of(grp * lanes + width, lanes)
        for b in range(nb):
            rows = pl.ds(b * step, step)
            keys = pl.ds(b * step, tall)
            flat = pl.ds(b * count, count)
            ok = (jnp.abs(qr[flat, :] - kr[b]) <= RADIUS) & (jnp.abs(qc[flat, :] - kc[b]) <= RADIUS)
            bias = jnp.where(ok, 0.0, -1e30)
            q8 = qkv_ref[rows, :, pl.ds(at, lanes)].reshape(count, lanes) * jnp.bfloat16(HDIM ** -0.5)
            g = g_ref[rows, :, pl.ds(at, lanes)].reshape(count, lanes)
            kb = ext[keys, :, pl.ds(at, lanes)].reshape(tall * slots, lanes)
            vb = ext[keys, :, pl.ds(at_v, lanes)].reshape(tall * slots, lanes)
            dqs, dks, dvs = [], [], []
            for h in range(2):
                part = slice(h * HDIM, (h + 1) * HDIM)
                qh, kh, vh, gh = q8[:, part], kb[:, part], vb[:, part], g[:, part]
                s = dot(qh, kh, nt) + bias
                ex = jnp.exp(s - jnp.max(s, axis=1, keepdims=True))
                p = ex * (1.0 / jnp.sum(ex, axis=1, keepdims=True))
                pb = p.astype(jnp.bfloat16)
                att = jnp.dot(pb, vh, preferred_element_type=jnp.float32)
                delta = jnp.sum(gh.astype(jnp.float32) * att, axis=1, keepdims=True)
                dp = dot(gh, vh, nt)
                ds = (p * (dp - delta)).astype(jnp.bfloat16)
                dqs.append(jnp.dot(ds, kh, preferred_element_type=jnp.float32) * (HDIM ** -0.5))
                dks.append(dot(ds, qh, tn))
                dvs.append(dot(pb, gh, tn))
            dq = jnp.concatenate(dqs, axis=1)
            if more is not None:
                more.turned[pl.ds(at, lanes), pl.ds(b * count, count)] = dq.T.astype(out_ref.dtype)
            out_ref[rows, :, pl.ds(at, lanes)] = dq.astype(out_ref.dtype).reshape(step, wide, lanes)
            both = jnp.concatenate(dks + dvs, axis=1).reshape(tall, slots, 2 * lanes)
            acc[grp, keys] += both
        for i, d in enumerate(DIRS):

            @pl.when(exists(d))
            def _():
                backward(i, grp).start()

        return carry

    lax.fori_loop(0, groups, one_group, 0)
    if more is not None:
        more.forward()

    def collect(grp, carry):
        for i, d in enumerate(DIRS):
            mine = own_pairs(d[0])
            here = pl.ds(half + mine.start, mine.size)

            @pl.when(exists(d))
            def _():
                backward_in(i, grp).wait_recv()
                if d[1] == 0:
                    acc[grp, here, pl.ds(0, wide)] += back[i][grp]
                else:
                    for r in range(2):
                        to = r * cols + (0 if d[1] < 0 else cols - side // 2)
                        acc[grp, here, pl.ds(to, side // 2)] += back[i][grp, :, pl.ds(r * side // 2, side // 2)]

        for j in range(2):
            to = pl.multiple_of(grp * lanes + (j + 1) * width, lanes)
            own = acc[grp, pl.ds(half, pairs), pl.ds(0, wide), pl.ds(j * lanes, lanes)]
            if more is not None:
                more.turned[pl.ds(to, lanes), :] = own.reshape(pairs * wide, lanes).T.astype(out_ref.dtype)
            out_ref[:, :, pl.ds(to, lanes)] = own.astype(out_ref.dtype)
        return carry

    lax.fori_loop(0, groups, collect, 0)
    if more is not None:
        more.finish()

    for i, d in enumerate(DIRS):

        @pl.when(exists(d))
        def _():
            forward(i).wait_send()
            for grp in range(groups):
                backward(i, grp).wait_send()


def halo_attention(qkv, first, last, g, qr, qc, kr, kc, slots, nn, ne):
    pairs, wide, total = qkv.shape
    half, width = RADIUS // 2, total // 3
    groups, side = width // 128, (slots - wide) // 2
    tall = pairs + 2 * half
    dma = pltpu.SemaphoreType.DMA
    vm = pl.BlockSpec(memory_space=pltpu.VMEM)
    back = [
        pltpu.VMEM((groups, half if dn else pairs, side if de else wide, 256), jnp.float32)
        for dn, de in DIRS
    ]
    return pl.pallas_call(
        functools.partial(halo_attention_kernel, nn, ne, None),
        out_shape=jax.ShapeDtypeStruct(qkv.shape, jnp.bfloat16),
        in_specs=[vm] * 8,
        out_specs=vm,
        scratch_shapes=[
            pltpu.VMEM((tall, slots, 2 * width), jnp.bfloat16),
            pltpu.VMEM((groups, tall, slots, 256), jnp.float32),
        ]
        + back
        + [dma((8,)), dma((8,)), dma((8, groups)), dma((8, groups))],
        compiler_params=pltpu.CompilerParams(
            collective_id=2, has_side_effects=True, vmem_limit_bytes=44 << 20
        ),
        cost_estimate=pl.CostEstimate(
            flops=14 * pairs * wide * tall * slots * width,
            bytes_accessed=4 << 20,
            transcendentals=pairs * wide * tall * slots * HEADS,
        ),
    )(qr, qc, kr, kc, qkv, first, last, g)


CH = 128


def weight_kernel(
    nn, ne, mid, tok_ref, dq_ref, out_ref, recv, part, slots,
    a_send, a_recv, r_send, r_recv, z_send, z_recv, p_send, p_recv, f_send, f_recv,
):
    e, n = lax.axis_index("ew"), lax.axis_index("ns")
    share = recv.shape[1]
    count = tok_ref.shape[0] // nn
    chunks = part.shape[0]
    owner = [min((c + 1) // 2, ne - 1) for c in range(chunks)]
    slot_of = [sum(1 for d in range(c) if owner[d] == owner[c]) for c in range(chunks)]
    core = lax.rem(n, 2)
    sibling = n + 1 - 2 * core

    def rows_of(d):
        return pl.ds(pl.multiple_of(d * share, 16), share)

    def at(d, m):
        return (d, m)

    def exchange(k):
        to = lax.rem(n + k, nn)
        return pltpu.make_async_remote_copy(
            src_ref=dq_ref.at[rows_of(to)], dst_ref=recv.at[n],
            send_sem=a_send.at[k], recv_sem=a_recv.at[n],
            device_id=at(e, to), device_id_type=MESH,
        )

    def arrived(k):
        src = lax.rem(n + nn - k, nn)
        return pltpu.make_async_remote_copy(
            src_ref=recv.at[src], dst_ref=recv.at[src],
            send_sem=a_send.at[k], recv_sem=a_recv.at[src],
            device_id=at(e, src), device_id_type=MESH,
        )

    for k in range(1, nn):
        exchange(k).start()
    recv[n] = dq_ref[rows_of(n), :]
    mid()
    for k in range(1, nn):
        arrived(k).wait_recv()

    def reduce_copy(c, src):
        return pltpu.make_async_remote_copy(
            src_ref=part.at[c], dst_ref=slots.at[slot_of[c], src],
            send_sem=r_send.at[c], recv_sem=r_recv.at[slot_of[c], src],
            device_id=at(owner[c], n), device_id_type=MESH,
        )

    order = [c for c in range(chunks)]
    for c in order:
        total = jnp.zeros((share, CH), jnp.float32)
        for s in range(nn):
            total += jnp.dot(
                recv[s], tok_ref[s * count : (s + 1) * count, c * CH : (c + 1) * CH],
                preferred_element_type=jnp.float32,
            )
        part[c] = total

        @pl.when(e != owner[c])
        def _():
            reduce_copy(c, e).start()

    def spot(c, m):
        return out_ref.at[rows_of(m), c * CH : (c + 1) * CH]

    def column_copy(c, k):
        return pltpu.make_async_remote_copy(
            src_ref=spot(c, n), dst_ref=spot(c, n),
            send_sem=z_send.at[c, k], recv_sem=z_recv.at[c],
            device_id=at(lax.rem(owner[c] + k, ne), n), device_id_type=MESH,
        )

    def plane_copy(c, m, to, sem, k, rsem):
        return pltpu.make_async_remote_copy(
            src_ref=spot(c, m), dst_ref=spot(c, m),
            send_sem=sem.at[c, k], recv_sem=rsem.at[c, m],
            device_id=at(e, to), device_id_type=MESH,
        )

    def peers(k):
        return lax.rem(n + 2 * k, nn)

    def spread(c):
        for k in range(1, nn // 2):
            plane_copy(c, n, peers(k), p_send, k, p_recv).start()
        plane_copy(c, n, sibling, p_send, 0, p_recv).start()

    for c in order:

        @pl.when(e == owner[c])
        def _():
            total = part[c]
            for k in range(1, ne):
                src = (owner[c] + k) % ne
                reduce_copy(c, src).wait_recv()
                total += slots[slot_of[c], src]
            out_ref[rows_of(n), c * CH : (c + 1) * CH] = total.astype(jnp.bfloat16)
            for k in range(1, ne):
                column_copy(c, k).start()
            spread(c)

    for c in order:

        @pl.when(e != owner[c])
        def _():
            column_copy(c, 1).wait_recv()
            spread(c)

    for c in order:
        for k in range(1, nn // 2):
            m = peers(k)
            plane_copy(c, m, sibling, p_send, 0, p_recv).wait_recv()
            plane_copy(c, m, sibling, f_send, k, f_recv).start()

    for c in order:
        plane_copy(c, sibling, sibling, p_send, 0, p_recv).wait_recv()
        for k in range(1, nn // 2):
            m = lax.rem(sibling + 2 * k, nn)
            plane_copy(c, m, sibling, f_send, k, f_recv).wait_recv()

    for k in range(1, nn):
        exchange(k).wait_send()
    for c in order:

        @pl.when(e != owner[c])
        def _():
            reduce_copy(c, e).wait_send()

        @pl.when(e == owner[c])
        def _():
            for k in range(1, ne):
                column_copy(c, k).wait_send()

        for k in range(nn // 2):
            plane_copy(c, n, sibling, p_send, k, p_recv).wait_send()
        for k in range(1, nn // 2):
            plane_copy(c, n, sibling, f_send, k, f_recv).wait_send()


class More:
    def __init__(self, nn, ne, tok, w, gt, gw, everything, dqkv, turned, sems, rest):
        self.nn, self.ne, self.tok, self.w, self.gt, self.gw = nn, ne, tok, w, gt, gw
        self.everything, self.dqkv, self.turned, self.rest = everything, dqkv, turned, rest
        self.t_send, self.t_recv, self.u_send, self.u_recv = sems
        self.e, self.n = lax.axis_index("ew"), lax.axis_index("ns")
        self.sibling = self.n + 1 - 2 * lax.rem(self.n, 2)
        self.count = tok.shape[0]

    def block(self, m):
        return pl.ds(pl.multiple_of(m * self.count, self.count), self.count)

    def peer(self, k, base=None):
        return self.sibling if k == 0 else lax.rem((self.n if base is None else base) + 2 * k, self.nn)

    def send(self, k):
        return pltpu.make_async_remote_copy(
            src_ref=self.tok, dst_ref=self.everything.at[self.block(self.n)],
            send_sem=self.t_send.at[k], recv_sem=self.t_recv.at[self.n],
            device_id=(self.e, self.peer(k)), device_id_type=MESH,
        )

    def pass_on(self, k, m, recv):
        return pltpu.make_async_remote_copy(
            src_ref=self.everything.at[self.block(m)], dst_ref=self.everything.at[self.block(m)],
            send_sem=self.u_send.at[k], recv_sem=recv.at[m],
            device_id=(self.e, self.sibling), device_id_type=MESH,
        )

    def start(self):
        for k in range(self.nn // 2):
            self.send(k).start()
        self.everything[self.block(self.n), :] = self.tok[...]

    def forward(self):
        for k in range(1, self.nn // 2):
            self.pass_on(k, self.peer(k), self.t_recv).wait_recv()
            self.pass_on(k, self.peer(k), self.u_recv).start()

    def mid(self):
        dq = self.dqkv[...].reshape(self.count, self.dqkv.shape[2])
        for c in range(0, self.w.shape[0], 256):
            self.gt[:, c : c + 256] = lax.dot_general(
                dq, self.w[c : c + 256, :], (((1,), (1,)), ((), ())), preferred_element_type=jnp.float32
            ).astype(jnp.bfloat16)
        self.pass_on(0, self.sibling, self.t_recv).wait_recv()
        for k in range(1, self.nn // 2):
            m = lax.rem(self.sibling + 2 * k, self.nn)
            self.pass_on(k, m, self.u_recv).wait_recv()

    def finish(self):
        weight_kernel(self.nn, self.ne, self.mid, self.everything, self.turned, self.gw, *self.rest)
        for k in range(self.nn // 2):
            self.send(k).wait_send()
        for k in range(1, self.nn // 2):
            self.pass_on(k, self.peer(k), self.u_recv).wait_send()


def fused_kernel(nn, ne, *refs):
    qr, qc, kr, kc, qkv, first, last, g, tok, w, gt, gw, everything, dqkv, turned = refs[:15]
    sems, scratch, rest = refs[15:19], refs[19:33], refs[33:]
    more = More(nn, ne, tok, w, gt, gw, everything, dqkv, turned, sems, rest)
    halo_attention_kernel(nn, ne, more, qr, qc, kr, kc, qkv, first, last, g, dqkv, *scratch)


def fused(qkv, first, last, g, qr, qc, kr, kc, slots, nn, ne, tok, w):
    pairs, wide, total = qkv.shape
    count, features = tok.shape
    half, width = RADIUS // 2, total // 3
    groups, side = width // 128, (slots - wide) // 2
    tall = pairs + 2 * half
    share, chunks = total // nn, features // CH
    dma = pltpu.SemaphoreType.DMA
    vm = pl.BlockSpec(memory_space=pltpu.VMEM)
    back = [
        pltpu.VMEM((groups, half if dn else pairs, side if de else wide, 256), jnp.float32)
        for dn, de in DIRS
    ]
    return pl.pallas_call(
        functools.partial(fused_kernel, nn, ne),
        out_shape=[
            jax.ShapeDtypeStruct((count, features), jnp.bfloat16),
            jax.ShapeDtypeStruct((total, features), jnp.bfloat16),
        ],
        in_specs=[vm] * 10,
        out_specs=[vm, vm],
        scratch_shapes=[
            pltpu.VMEM((nn * count, features), jnp.bfloat16),
            pltpu.VMEM((pairs, wide, total), jnp.bfloat16),
            pltpu.VMEM((total, count), jnp.bfloat16),
            dma((nn // 2,)), dma((nn,)), dma((nn // 2,)), dma((nn,)),
            pltpu.VMEM((tall, slots, 2 * width), jnp.bfloat16),
            pltpu.VMEM((groups, tall, slots, 256), jnp.float32),
        ]
        + back
        + [
            dma((8,)), dma((8,)), dma((8, groups)), dma((8, groups)),
            pltpu.VMEM((nn, share, count), jnp.bfloat16),
            pltpu.VMEM((chunks, share, CH), jnp.float32),
            pltpu.VMEM((2, ne, share, CH), jnp.float32),
            dma((nn,)), dma((nn,)),
            dma((chunks,)), dma((2, ne)),
            dma((chunks, ne)), dma((chunks,)),
            dma((chunks, nn // 2)), dma((chunks, nn)),
            dma((chunks, nn // 2)), dma((chunks, nn)),
        ],
        compiler_params=pltpu.CompilerParams(
            collective_id=1, has_side_effects=True, vmem_limit_bytes=44 << 20
        ),
        cost_estimate=pl.CostEstimate(
            flops=14 * pairs * wide * tall * slots * width + 4 * count * features * total,
            bytes_accessed=8 << 20,
            transcendentals=pairs * wide * tall * slots * HEADS,
        ),
    )(qr, qc, kr, kc, qkv, first, last, g, tok, w)


def local(tokens, w_qkv, grad_out):
    tile_rows, tile_cols, features = tokens.shape
    nn, ne = lax.axis_size("ns"), lax.axis_size("ew")
    width = w_qkv.shape[1] // 3
    count = tile_rows * tile_cols
    flat_tokens = tokens.reshape(count, features)
    paired = nn == 8 and ne == 4
    projected = jnp.dot(flat_tokens, w_qkv, preferred_element_type=jnp.float32).astype(jnp.bfloat16)
    half, pairs, wide, edge = RADIUS // 2, tile_rows // 2, 2 * tile_cols, 8
    slots = wide + 4 * edge
    qkv = projected.reshape(pairs, wide, 3 * width)
    by_row = projected[:, width:].reshape(tile_rows, tile_cols, 2 * width)
    first = by_row[:, :edge].reshape(pairs, 2 * edge, 2 * width)
    last = by_row[:, tile_cols - edge :].reshape(pairs, 2 * edge, 2 * width)
    nb = 2
    row0 = lax.axis_index("ns") * tile_rows
    col0 = lax.axis_index("ew") * tile_cols
    qi = jnp.arange(count, dtype=jnp.int32)
    qr = (row0 + qi // tile_cols)[:, None]
    qc = (col0 + qi % tile_cols)[:, None]
    slot = np.arange(slots)
    in_side = np.maximum(slot - wide, 0)
    slot_row = np.where(slot < wide, slot // tile_cols, (in_side % (2 * edge)) // edge)
    slot_col = np.where(
        slot < wide,
        slot % tile_cols,
        np.where(in_side < 2 * edge, tile_cols + in_side % edge, in_side % edge - edge),
    )
    ext_row = (2 * np.arange(pairs + 2 * half)[:, None] - RADIUS + slot_row[None]).astype(np.int32)
    ext_col = np.broadcast_to(slot_col[None], ext_row.shape).astype(np.int32)
    kr, kc = row0 + ext_row, col0 + ext_col
    inside = (kr >= 0) & (kr < nn * tile_rows) & (kc >= 0) & (kc < ne * tile_cols)
    kr = jnp.where(inside, kr, -1000)
    per = pairs // nb
    pick = lambda a: jnp.stack([a[b * per : b * per + per + 2 * half].reshape(1, -1) for b in range(nb)])
    halo_args = (
        qkv, first, last, grad_out.reshape(pairs, wide, width), qr, qc, pick(kr), pick(kc), slots, nn, ne
    )
    if paired:
        grad_tokens, grad_w_t = fused(*halo_args, flat_tokens, w_qkv)
        return (grad_tokens.reshape(tokens.shape), grad_w_t.T)
    dqkv = halo_attention(*halo_args).reshape(count, 3 * width)
    grad_tokens = (
        jnp.dot(dqkv, w_qkv.T, preferred_element_type=jnp.float32)
        .astype(jnp.bfloat16)
        .reshape(tile_rows, tile_cols, features)
    )
    weight_part = lax.dot_general(
        flat_tokens, dqkv, (((0,), (0,)), ((), ())), preferred_element_type=jnp.float32
    )
    grad_w = lax.psum(weight_part, ("ew", "ns")).astype(jnp.bfloat16)
    return (grad_tokens, grad_w)


def solution(mesh):
    in_specs = (P("ns", "ew", None), P(), P("ns", "ew", None))
    out_specs = (P("ns", "ew", None), P())
    return jax.shard_map(local, mesh=mesh, in_specs=in_specs, out_specs=out_specs, check_vma=False)
```

```python
import functools

import jax
import jax.numpy as jnp
import numpy as np
from jax import lax
from jax.experimental import pallas as pl
from jax.experimental.pallas import tpu as pltpu
from jax.sharding import PartitionSpec as P

HEADS = 6
HDIM = 64
RADIUS = 6
MESH = pl.DeviceIdType.MESH


DIRS = [(dn, de) for dn in (-1, 0, 1) for de in (-1, 0, 1) if (dn, de) != (0, 0)]


def halo_attention_kernel(
    nn, ne, more, qr, qc, kr, kc, qkv_ref, first_ref, last_ref, g_ref, out_ref, ext, acc, *rest
):
    back = rest[:8]
    f_send, f_recv, b_send, b_recv = rest[8:]
    e, n = lax.axis_index("ew"), lax.axis_index("ns")
    pairs, wide, total = qkv_ref.shape
    width = total // 3
    half = RADIUS // 2
    groups, lanes = width // 128, 128
    slots = ext.shape[1]
    side = (slots - wide) // 2
    nb = kr.shape[0]
    step = pairs // nb
    tall = step + 2 * half
    cols = wide // 2

    def exists(d):
        dn, de = d
        return (n + dn >= 0) & (n + dn < nn) & (e + de >= 0) & (e + de < ne)

    def own_pairs(dn):
        return {-1: pl.ds(0, half), 0: pl.ds(0, pairs), 1: pl.ds(pairs - half, half)}[dn]

    def region(d):
        rows = {-1: pl.ds(0, half), 0: pl.ds(half, pairs), 1: pl.ds(half + pairs, half)}[d[0]]
        place = {0: pl.ds(0, wide), 1: pl.ds(wide, side), -1: pl.ds(wide + side, side)}[d[1]]
        return rows, place

    def opposite(i):
        return DIRS.index((-DIRS[i][0], -DIRS[i][1]))

    def forward(i):
        dn, de = DIRS[i]
        rows = own_pairs(dn)
        if de == 0:
            src = qkv_ref.at[rows, :, pl.ds(width, 2 * width)]
        else:
            src = (first_ref if de < 0 else last_ref).at[rows]
        there = opposite(i)
        a, b = region(DIRS[there])
        return pltpu.make_async_remote_copy(
            src_ref=src, dst_ref=ext.at[a, b], send_sem=f_send.at[i], recv_sem=f_recv.at[there],
            device_id=(e + de, n + dn), device_id_type=MESH,
        )

    def forward_in(i):
        a, b = region(DIRS[i])
        return pltpu.make_async_remote_copy(
            src_ref=ext.at[a, b], dst_ref=ext.at[a, b], send_sem=f_send.at[i], recv_sem=f_recv.at[i],
            device_id=(e + DIRS[i][1], n + DIRS[i][0]), device_id_type=MESH,
        )

    def backward(i, grp):
        a, b = region(DIRS[i])
        there = opposite(i)
        return pltpu.make_async_remote_copy(
            src_ref=acc.at[grp, a, b], dst_ref=back[there].at[grp],
            send_sem=b_send.at[i, grp], recv_sem=b_recv.at[there, grp],
            device_id=(e + DIRS[i][1], n + DIRS[i][0]), device_id_type=MESH,
        )

    def backward_in(i, grp):
        return pltpu.make_async_remote_copy(
            src_ref=back[i].at[grp], dst_ref=back[i].at[grp],
            send_sem=b_send.at[i, grp], recv_sem=b_recv.at[i, grp],
            device_id=(e + DIRS[i][1], n + DIRS[i][0]), device_id_type=MESH,
        )

    near = DIRS
    barrier = pltpu.get_barrier_semaphore()
    if more is not None:
        near = [d for d in DIRS if d[0] and d[1]]
        for k in range(1, nn):
            pl.semaphore_signal(barrier, inc=1, device_id=(e, lax.rem(n + k, nn)), device_id_type=MESH)
        for k in range(1, ne):
            pl.semaphore_signal(barrier, inc=1, device_id=(lax.rem(e + k, ne), n), device_id_type=MESH)
    for d in near:

        @pl.when(exists(d))
        def _():
            pl.semaphore_signal(barrier, inc=1, device_id=(e + d[1], n + d[0]), device_id_type=MESH)

    others = nn - 1 + ne - 1 if more is not None else 0
    pl.semaphore_wait(barrier, others + sum(exists(d).astype(jnp.int32) for d in near))

    for i, d in enumerate(DIRS):

        @pl.when(exists(d))
        def _():
            forward(i).start()

    ext[pl.ds(half, pairs), pl.ds(0, wide), :] = qkv_ref[:, :, pl.ds(width, 2 * width)]
    acc[...] = jnp.zeros_like(acc)
    for i, d in enumerate(DIRS):
        a, b = region(d)

        @pl.when(jnp.logical_not(exists(d)))
        def _():
            ext[a, b, :] = jnp.zeros((a.size, b.size, 2 * width), ext.dtype)

        @pl.when(exists(d))
        def _():
            forward_in(i).wait_recv()

    if more is not None:
        more.start()
    nt = (((1,), (1,)), ((), ()))
    tn = (((0,), (0,)), ((), ()))
    dot = functools.partial(lax.dot_general, preferred_element_type=jnp.float32)
    count = step * wide

    def one_group(grp, carry):
        at = pl.multiple_of(grp * lanes, lanes)
        at_v = pl.multiple_of(grp * lanes + width, lanes)
        for b in range(nb):
            rows = pl.ds(b * step, step)
            keys = pl.ds(b * step, tall)
            flat = pl.ds(b * count, count)
            ok = (jnp.abs(qr[flat, :] - kr[b]) <= RADIUS) & (jnp.abs(qc[flat, :] - kc[b]) <= RADIUS)
            bias = jnp.where(ok, 0.0, -1e30)
            q8 = qkv_ref[rows, :, pl.ds(at, lanes)].reshape(count, lanes) * jnp.bfloat16(HDIM ** -0.5)
            g = g_ref[rows, :, pl.ds(at, lanes)].reshape(count, lanes)
            kb = ext[keys, :, pl.ds(at, lanes)].reshape(tall * slots, lanes)
            vb = ext[keys, :, pl.ds(at_v, lanes)].reshape(tall * slots, lanes)
            dqs, dks, dvs = [], [], []
            for h in range(2):
                part = slice(h * HDIM, (h + 1) * HDIM)
                qh, kh, vh, gh = q8[:, part], kb[:, part], vb[:, part], g[:, part]
                s = dot(qh, kh, nt) + bias
                ex = jnp.exp(s - jnp.max(s, axis=1, keepdims=True))
                p = ex * (1.0 / jnp.sum(ex, axis=1, keepdims=True))
                pb = p.astype(jnp.bfloat16)
                att = jnp.dot(pb, vh, preferred_element_type=jnp.float32)
                delta = jnp.sum(gh.astype(jnp.float32) * att, axis=1, keepdims=True)
                dp = dot(gh, vh, nt)
                ds = (p * (dp - delta)).astype(jnp.bfloat16)
                dqs.append(jnp.dot(ds, kh, preferred_element_type=jnp.float32) * (HDIM ** -0.5))
                dks.append(dot(ds, qh, tn))
                dvs.append(dot(pb, gh, tn))
            dq = jnp.concatenate(dqs, axis=1)
            if more is not None:
                more.turned[pl.ds(at, lanes), pl.ds(b * count, count)] = dq.T.astype(out_ref.dtype)
            out_ref[rows, :, pl.ds(at, lanes)] = dq.astype(out_ref.dtype).reshape(step, wide, lanes)
            both = jnp.concatenate(dks + dvs, axis=1).reshape(tall, slots, 2 * lanes)
            acc[grp, keys] += both
        for i, d in enumerate(DIRS):

            @pl.when(exists(d))
            def _():
                backward(i, grp).start()

        return carry

    lax.fori_loop(0, groups, one_group, 0)
    if more is not None:
        more.early()

    def collect(grp, carry):
        for i, d in enumerate(DIRS):
            mine = own_pairs(d[0])
            here = pl.ds(half + mine.start, mine.size)

            @pl.when(exists(d))
            def _():
                backward_in(i, grp).wait_recv()
                if d[1] == 0:
                    acc[grp, here, pl.ds(0, wide)] += back[i][grp]
                else:
                    for r in range(2):
                        to = r * cols + (0 if d[1] < 0 else cols - side // 2)
                        acc[grp, here, pl.ds(to, side // 2)] += back[i][grp, :, pl.ds(r * side // 2, side // 2)]

        for j in range(2):
            to = pl.multiple_of(grp * lanes + (j + 1) * width, lanes)
            own = acc[grp, pl.ds(half, pairs), pl.ds(0, wide), pl.ds(j * lanes, lanes)]
            if more is not None:
                more.turned[pl.ds(to, lanes), :] = own.reshape(pairs * wide, lanes).T.astype(out_ref.dtype)
            out_ref[:, :, pl.ds(to, lanes)] = own.astype(out_ref.dtype)
        return carry

    lax.fori_loop(0, groups, collect, 0)
    if more is not None:
        more.finish()

    for i, d in enumerate(DIRS):

        @pl.when(exists(d))
        def _():
            forward(i).wait_send()
            for grp in range(groups):
                backward(i, grp).wait_send()


def halo_attention(qkv, first, last, g, qr, qc, kr, kc, slots, nn, ne):
    pairs, wide, total = qkv.shape
    half, width = RADIUS // 2, total // 3
    groups, side = width // 128, (slots - wide) // 2
    tall = pairs + 2 * half
    dma = pltpu.SemaphoreType.DMA
    vm = pl.BlockSpec(memory_space=pltpu.VMEM)
    back = [
        pltpu.VMEM((groups, half if dn else pairs, side if de else wide, 256), jnp.float32)
        for dn, de in DIRS
    ]
    return pl.pallas_call(
        functools.partial(halo_attention_kernel, nn, ne, None),
        out_shape=jax.ShapeDtypeStruct(qkv.shape, jnp.bfloat16),
        in_specs=[vm] * 8,
        out_specs=vm,
        scratch_shapes=[
            pltpu.VMEM((tall, slots, 2 * width), jnp.bfloat16),
            pltpu.VMEM((groups, tall, slots, 256), jnp.float32),
        ]
        + back
        + [dma((8,)), dma((8,)), dma((8, groups)), dma((8, groups))],
        compiler_params=pltpu.CompilerParams(
            collective_id=2, has_side_effects=True, vmem_limit_bytes=44 << 20
        ),
        cost_estimate=pl.CostEstimate(
            flops=14 * pairs * wide * tall * slots * width,
            bytes_accessed=4 << 20,
            transcendentals=pairs * wide * tall * slots * HEADS,
        ),
    )(qr, qc, kr, kc, qkv, first, last, g)


CH = 128


def weight_kernel(
    nn, ne, base, tok_ref, dq_ref, out_ref, recv, part, slots,
    a_send, a_recv, r_send, r_recv, z_send, z_recv, p_send, p_recv, f_send, f_recv,
):
    e, n = lax.axis_index("ew"), lax.axis_index("ns")
    share = recv.shape[1]
    count = tok_ref.shape[0] // nn
    chunks = part.shape[0]
    owner = [min((c + 1) // 2, ne - 1) for c in range(chunks)]
    slot_of = [sum(1 for d in range(c) if owner[d] == owner[c]) for c in range(chunks)]
    core = lax.rem(n, 2)
    sibling = n + 1 - 2 * core

    def rows_of(d):
        return pl.ds(pl.multiple_of(base + d * share, 16), share)

    def at(d, m):
        return (d, m)

    def exchange(k):
        to = lax.rem(n + k, nn)
        return pltpu.make_async_remote_copy(
            src_ref=dq_ref.at[rows_of(to)], dst_ref=recv.at[n],
            send_sem=a_send.at[k], recv_sem=a_recv.at[n],
            device_id=at(e, to), device_id_type=MESH,
        )

    def arrived(k):
        src = lax.rem(n + nn - k, nn)
        return pltpu.make_async_remote_copy(
            src_ref=recv.at[src], dst_ref=recv.at[src],
            send_sem=a_send.at[k], recv_sem=a_recv.at[src],
            device_id=at(e, src), device_id_type=MESH,
        )

    for k in range(1, nn):
        exchange(k).start()
    recv[n] = dq_ref[rows_of(n), :]
    yield
    for k in range(1, nn):
        arrived(k).wait_recv()

    def reduce_copy(c, src):
        return pltpu.make_async_remote_copy(
            src_ref=part.at[c], dst_ref=slots.at[slot_of[c], src],
            send_sem=r_send.at[c], recv_sem=r_recv.at[slot_of[c], src],
            device_id=at(owner[c], n), device_id_type=MESH,
        )

    order = [c for c in range(chunks)]
    for c in order:
        total = jnp.zeros((share, CH), jnp.float32)
        for s in range(nn):
            total += jnp.dot(
                recv[s], tok_ref[s * count : (s + 1) * count, c * CH : (c + 1) * CH],
                preferred_element_type=jnp.float32,
            )
        part[c] = total

        @pl.when(e != owner[c])
        def _():
            reduce_copy(c, e).start()

    yield

    def spot(c, m):
        return out_ref.at[rows_of(m), c * CH : (c + 1) * CH]

    def column_copy(c, k):
        return pltpu.make_async_remote_copy(
            src_ref=spot(c, n), dst_ref=spot(c, n),
            send_sem=z_send.at[c, k], recv_sem=z_recv.at[c],
            device_id=at(lax.rem(owner[c] + k, ne), n), device_id_type=MESH,
        )

    def plane_copy(c, m, to, sem, k, rsem):
        return pltpu.make_async_remote_copy(
            src_ref=spot(c, m), dst_ref=spot(c, m),
            send_sem=sem.at[c, k], recv_sem=rsem.at[c, m],
            device_id=at(e, to), device_id_type=MESH,
        )

    def peers(k):
        return lax.rem(n + 2 * k, nn)

    def spread(c):
        for k in range(1, nn // 2):
            plane_copy(c, n, peers(k), p_send, k, p_recv).start()
        plane_copy(c, n, sibling, p_send, 0, p_recv).start()

    for c in order:

        @pl.when(e == owner[c])
        def _():
            total = part[c]
            for k in range(1, ne):
                src = (owner[c] + k) % ne
                reduce_copy(c, src).wait_recv()
                total += slots[slot_of[c], src]
            out_ref[rows_of(n), c * CH : (c + 1) * CH] = total.astype(jnp.bfloat16)
            for k in range(1, ne):
                column_copy(c, k).start()
            spread(c)

    yield
    for c in order:

        @pl.when(e != owner[c])
        def _():
            column_copy(c, 1).wait_recv()
            spread(c)

    yield
    for c in order:
        for k in range(1, nn // 2):
            m = peers(k)
            plane_copy(c, m, sibling, p_send, 0, p_recv).wait_recv()
            plane_copy(c, m, sibling, f_send, k, f_recv).start()

    yield
    for c in order:
        plane_copy(c, sibling, sibling, p_send, 0, p_recv).wait_recv()
        for k in range(1, nn // 2):
            m = lax.rem(sibling + 2 * k, nn)
            plane_copy(c, m, sibling, f_send, k, f_recv).wait_recv()

    for k in range(1, nn):
        exchange(k).wait_send()
    for c in order:

        @pl.when(e != owner[c])
        def _():
            reduce_copy(c, e).wait_send()

        @pl.when(e == owner[c])
        def _():
            for k in range(1, ne):
                column_copy(c, k).wait_send()

        for k in range(nn // 2):
            plane_copy(c, n, sibling, p_send, k, p_recv).wait_send()
        for k in range(1, nn // 2):
            plane_copy(c, n, sibling, f_send, k, f_recv).wait_send()


class More:
    def __init__(self, nn, ne, tok, w, gt, gw, everything, dqkv, turned, sems, rest):
        self.nn, self.ne, self.tok, self.w, self.gt, self.gw = nn, ne, tok, w, gt, gw
        self.everything, self.dqkv, self.turned, self.rest = everything, dqkv, turned, rest
        self.t_send, self.t_recv, self.u_send, self.u_recv = sems
        self.e, self.n = lax.axis_index("ew"), lax.axis_index("ns")
        self.sibling = self.n + 1 - 2 * lax.rem(self.n, 2)
        self.count = tok.shape[0]

    def block(self, m):
        return pl.ds(pl.multiple_of(m * self.count, self.count), self.count)

    def peer(self, k, base=None):
        return self.sibling if k == 0 else lax.rem((self.n if base is None else base) + 2 * k, self.nn)

    def send(self, k):
        return pltpu.make_async_remote_copy(
            src_ref=self.tok, dst_ref=self.everything.at[self.block(self.n)],
            send_sem=self.t_send.at[k], recv_sem=self.t_recv.at[self.n],
            device_id=(self.e, self.peer(k)), device_id_type=MESH,
        )

    def pass_on(self, k, m, recv):
        return pltpu.make_async_remote_copy(
            src_ref=self.everything.at[self.block(m)], dst_ref=self.everything.at[self.block(m)],
            send_sem=self.u_send.at[k], recv_sem=recv.at[m],
            device_id=(self.e, self.sibling), device_id_type=MESH,
        )

    def start(self):
        for k in range(self.nn // 2):
            self.send(k).start()
        self.everything[self.block(self.n), :] = self.tok[...]

    def forward(self):
        for k in range(1, self.nn // 2):
            self.pass_on(k, self.peer(k), self.t_recv).wait_recv()
            self.pass_on(k, self.peer(k), self.u_recv).start()

    def early(self):
        half = len(self.rest) // 2
        width = self.turned.shape[0] // 3
        make = lambda base, rest: weight_kernel(
            self.nn, self.ne, base, self.everything, self.turned, self.gw, *rest
        )
        self.parts = [make(0, self.rest[:half]), make(width, self.rest[half:])]
        next(self.parts[0])
        self.forward()

    def tokens_in(self):
        self.pass_on(0, self.sibling, self.t_recv).wait_recv()
        for k in range(1, self.nn // 2):
            m = lax.rem(self.sibling + 2 * k, self.nn)
            self.pass_on(k, m, self.u_recv).wait_recv()

    def mid(self):
        dq = self.dqkv[...].reshape(self.count, self.dqkv.shape[2])
        for c in range(0, self.w.shape[0], 256):
            self.gt[:, c : c + 256] = lax.dot_general(
                dq, self.w[c : c + 256, :], (((1,), (1,)), ((), ())), preferred_element_type=jnp.float32
            ).astype(jnp.bfloat16)

    def finish(self):
        first, second = self.parts
        next(second)
        self.tokens_in()
        next(first)
        self.mid()
        next(second)
        for _ in range(3):
            next(first)
            next(second)
        next(first, None)
        next(second, None)
        for k in range(self.nn // 2):
            self.send(k).wait_send()
        for k in range(1, self.nn // 2):
            self.pass_on(k, self.peer(k), self.u_recv).wait_send()


def fused_kernel(nn, ne, *refs):
    qr, qc, kr, kc, qkv, first, last, g, tok, w, gt, gw, everything, dqkv, turned = refs[:15]
    sems, scratch, rest = refs[15:19], refs[19:33], refs[33:]
    more = More(nn, ne, tok, w, gt, gw, everything, dqkv, turned, sems, rest)
    halo_attention_kernel(nn, ne, more, qr, qc, kr, kc, qkv, first, last, g, dqkv, *scratch)


def fused(qkv, first, last, g, qr, qc, kr, kc, slots, nn, ne, tok, w):
    pairs, wide, total = qkv.shape
    count, features = tok.shape
    half, width = RADIUS // 2, total // 3
    groups, side = width // 128, (slots - wide) // 2
    tall = pairs + 2 * half
    chunks = features // CH
    dma = pltpu.SemaphoreType.DMA

    def weight_scratch(share):
        return [
            pltpu.VMEM((nn, share, count), jnp.bfloat16),
            pltpu.VMEM((chunks, share, CH), jnp.float32),
            pltpu.VMEM((2, ne, share, CH), jnp.float32),
            dma((nn,)), dma((nn,)),
            dma((chunks,)), dma((2, ne)),
            dma((chunks, ne)), dma((chunks,)),
            dma((chunks, nn // 2)), dma((chunks, nn)),
            dma((chunks, nn // 2)), dma((chunks, nn)),
        ]

    vm = pl.BlockSpec(memory_space=pltpu.VMEM)
    back = [
        pltpu.VMEM((groups, half if dn else pairs, side if de else wide, 256), jnp.float32)
        for dn, de in DIRS
    ]
    return pl.pallas_call(
        functools.partial(fused_kernel, nn, ne),
        out_shape=[
            jax.ShapeDtypeStruct((count, features), jnp.bfloat16),
            jax.ShapeDtypeStruct((total, features), jnp.bfloat16),
        ],
        in_specs=[vm] * 10,
        out_specs=[vm, vm],
        scratch_shapes=[
            pltpu.VMEM((nn * count, features), jnp.bfloat16),
            pltpu.VMEM((pairs, wide, total), jnp.bfloat16),
            pltpu.VMEM((total, count), jnp.bfloat16),
            dma((nn // 2,)), dma((nn,)), dma((nn // 2,)), dma((nn,)),
            pltpu.VMEM((tall, slots, 2 * width), jnp.bfloat16),
            pltpu.VMEM((groups, tall, slots, 256), jnp.float32),
        ]
        + back
        + [
            dma((8,)), dma((8,)), dma((8, groups)), dma((8, groups)),
        ]
        + weight_scratch(width // nn)
        + weight_scratch(2 * width // nn),
        compiler_params=pltpu.CompilerParams(
            collective_id=1, has_side_effects=True, vmem_limit_bytes=44 << 20
        ),
        cost_estimate=pl.CostEstimate(
            flops=14 * pairs * wide * tall * slots * width + 4 * count * features * total,
            bytes_accessed=8 << 20,
            transcendentals=pairs * wide * tall * slots * HEADS,
        ),
    )(qr, qc, kr, kc, qkv, first, last, g, tok, w)


def local(tokens, w_qkv, grad_out):
    tile_rows, tile_cols, features = tokens.shape
    nn, ne = lax.axis_size("ns"), lax.axis_size("ew")
    width = w_qkv.shape[1] // 3
    count = tile_rows * tile_cols
    flat_tokens = tokens.reshape(count, features)
    paired = nn == 8 and ne == 4
    projected = jnp.dot(flat_tokens, w_qkv, preferred_element_type=jnp.float32).astype(jnp.bfloat16)
    half, pairs, wide, edge = RADIUS // 2, tile_rows // 2, 2 * tile_cols, 8
    slots = wide + 4 * edge
    qkv = projected.reshape(pairs, wide, 3 * width)
    by_row = projected[:, width:].reshape(tile_rows, tile_cols, 2 * width)
    first = by_row[:, :edge].reshape(pairs, 2 * edge, 2 * width)
    last = by_row[:, tile_cols - edge :].reshape(pairs, 2 * edge, 2 * width)
    nb = 2
    row0 = lax.axis_index("ns") * tile_rows
    col0 = lax.axis_index("ew") * tile_cols
    qi = jnp.arange(count, dtype=jnp.int32)
    qr = (row0 + qi // tile_cols)[:, None]
    qc = (col0 + qi % tile_cols)[:, None]
    slot = np.arange(slots)
    in_side = np.maximum(slot - wide, 0)
    slot_row = np.where(slot < wide, slot // tile_cols, (in_side % (2 * edge)) // edge)
    slot_col = np.where(
        slot < wide,
        slot % tile_cols,
        np.where(in_side < 2 * edge, tile_cols + in_side % edge, in_side % edge - edge),
    )
    ext_row = (2 * np.arange(pairs + 2 * half)[:, None] - RADIUS + slot_row[None]).astype(np.int32)
    ext_col = np.broadcast_to(slot_col[None], ext_row.shape).astype(np.int32)
    kr, kc = row0 + ext_row, col0 + ext_col
    inside = (kr >= 0) & (kr < nn * tile_rows) & (kc >= 0) & (kc < ne * tile_cols)
    kr = jnp.where(inside, kr, -1000)
    per = pairs // nb
    pick = lambda a: jnp.stack([a[b * per : b * per + per + 2 * half].reshape(1, -1) for b in range(nb)])
    halo_args = (
        qkv, first, last, grad_out.reshape(pairs, wide, width), qr, qc, pick(kr), pick(kc), slots, nn, ne
    )
    if paired:
        grad_tokens, grad_w_t = fused(*halo_args, flat_tokens, w_qkv)
        return (grad_tokens.reshape(tokens.shape), grad_w_t.T)
    dqkv = halo_attention(*halo_args).reshape(count, 3 * width)
    grad_tokens = (
        jnp.dot(dqkv, w_qkv.T, preferred_element_type=jnp.float32)
        .astype(jnp.bfloat16)
        .reshape(tile_rows, tile_cols, features)
    )
    weight_part = lax.dot_general(
        flat_tokens, dqkv, (((0,), (0,)), ((), ())), preferred_element_type=jnp.float32
    )
    grad_w = lax.psum(weight_part, ("ew", "ns")).astype(jnp.bfloat16)
    return (grad_tokens, grad_w)


def solution(mesh):
    in_specs = (P("ns", "ew", None), P(), P("ns", "ew", None))
    out_specs = (P("ns", "ew", None), P())
    return jax.shard_map(local, mesh=mesh, in_specs=in_specs, out_specs=out_specs, check_vma=False)
```

```python
import functools

import jax
import jax.numpy as jnp
import numpy as np
from jax import lax
from jax.experimental import pallas as pl
from jax.experimental.pallas import tpu as pltpu
from jax.sharding import PartitionSpec as P

HEADS = 6
HDIM = 64
RADIUS = 6
MESH = pl.DeviceIdType.MESH


DIRS = [(dn, de) for dn in (-1, 0, 1) for de in (-1, 0, 1) if (dn, de) != (0, 0)]


def halo_attention_kernel(
    nn, ne, more, qr, qc, kr, kc, qkv_ref, first_ref, last_ref, g_ref, out_ref, ext, acc, *rest
):
    back = rest[:8]
    f_send, f_recv, b_send, b_recv = rest[8:]
    e, n = lax.axis_index("ew"), lax.axis_index("ns")
    pairs, wide, total = qkv_ref.shape
    width = total // 3
    half = RADIUS // 2
    groups, lanes = width // 128, 128
    slots = ext.shape[1]
    side = (slots - wide) // 2
    nb = kr.shape[0]
    step = pairs // nb
    tall = step + 2 * half
    cols = wide // 2

    def exists(d):
        dn, de = d
        return (n + dn >= 0) & (n + dn < nn) & (e + de >= 0) & (e + de < ne)

    def own_pairs(dn):
        return {-1: pl.ds(0, half), 0: pl.ds(0, pairs), 1: pl.ds(pairs - half, half)}[dn]

    def region(d):
        rows = {-1: pl.ds(0, half), 0: pl.ds(half, pairs), 1: pl.ds(half + pairs, half)}[d[0]]
        place = {0: pl.ds(0, wide), 1: pl.ds(wide, side), -1: pl.ds(wide + side, side)}[d[1]]
        return rows, place

    def opposite(i):
        return DIRS.index((-DIRS[i][0], -DIRS[i][1]))

    def lane(grp, j, start=0):
        return pl.ds(pl.multiple_of(start + j * width + grp * lanes, lanes), lanes)

    def forward(i, grp, j):
        dn, de = DIRS[i]
        rows = own_pairs(dn)
        if de == 0:
            src = qkv_ref.at[rows, :, lane(grp, j, width)]
        else:
            src = (first_ref if de < 0 else last_ref).at[rows, :, lane(grp, j)]
        there = opposite(i)
        a, b = region(DIRS[there])
        return pltpu.make_async_remote_copy(
            src_ref=src, dst_ref=ext.at[a, b, lane(grp, j)],
            send_sem=f_send.at[i, grp, j], recv_sem=f_recv.at[there, grp, j],
            device_id=(e + de, n + dn), device_id_type=MESH,
        )

    def forward_in(i, grp, j):
        a, b = region(DIRS[i])
        here = ext.at[a, b, lane(grp, j)]
        return pltpu.make_async_remote_copy(
            src_ref=here, dst_ref=here, send_sem=f_send.at[i, grp, j], recv_sem=f_recv.at[i, grp, j],
            device_id=(e + DIRS[i][1], n + DIRS[i][0]), device_id_type=MESH,
        )

    def strips_in(grp):
        for i, d in enumerate(DIRS):

            @pl.when(exists(d))
            def _():
                for j in range(2):
                    forward_in(i, grp, j).wait_recv()

    def backward(i, grp):
        a, b = region(DIRS[i])
        there = opposite(i)
        return pltpu.make_async_remote_copy(
            src_ref=acc.at[grp, a, b], dst_ref=back[there].at[grp],
            send_sem=b_send.at[i, grp], recv_sem=b_recv.at[there, grp],
            device_id=(e + DIRS[i][1], n + DIRS[i][0]), device_id_type=MESH,
        )

    def backward_in(i, grp):
        return pltpu.make_async_remote_copy(
            src_ref=back[i].at[grp], dst_ref=back[i].at[grp],
            send_sem=b_send.at[i, grp], recv_sem=b_recv.at[i, grp],
            device_id=(e + DIRS[i][1], n + DIRS[i][0]), device_id_type=MESH,
        )

    near = DIRS
    barrier = pltpu.get_barrier_semaphore()
    if more is not None:
        near = [d for d in DIRS if d[0] and d[1]]
        for k in range(1, nn):
            pl.semaphore_signal(barrier, inc=1, device_id=(e, lax.rem(n + k, nn)), device_id_type=MESH)
        for k in range(1, ne):
            pl.semaphore_signal(barrier, inc=1, device_id=(lax.rem(e + k, ne), n), device_id_type=MESH)
    for d in near:

        @pl.when(exists(d))
        def _():
            pl.semaphore_signal(barrier, inc=1, device_id=(e + d[1], n + d[0]), device_id_type=MESH)

    others = nn - 1 + ne - 1 if more is not None else 0
    pl.semaphore_wait(barrier, others + sum(exists(d).astype(jnp.int32) for d in near))

    for grp in range(groups):
        for i, d in enumerate(DIRS):

            @pl.when(exists(d))
            def _():
                for j in range(2):
                    forward(i, grp, j).start()

    ext[pl.ds(half, pairs), pl.ds(0, wide), :] = qkv_ref[:, :, pl.ds(width, 2 * width)]
    acc[...] = jnp.zeros_like(acc)
    for i, d in enumerate(DIRS):
        a, b = region(d)

        @pl.when(jnp.logical_not(exists(d)))
        def _():
            ext[a, b, :] = jnp.zeros((a.size, b.size, 2 * width), ext.dtype)

    strips_in(0)
    if more is not None:
        more.start()
    nt = (((1,), (1,)), ((), ()))
    tn = (((0,), (0,)), ((), ()))
    dot = functools.partial(lax.dot_general, preferred_element_type=jnp.float32)
    count = step * wide

    def one_group(grp, carry):
        @pl.when(grp > 0)
        def _():
            strips_in(grp)

        at = pl.multiple_of(grp * lanes, lanes)
        at_v = pl.multiple_of(grp * lanes + width, lanes)
        for b in range(nb):
            rows = pl.ds(b * step, step)
            keys = pl.ds(b * step, tall)
            flat = pl.ds(b * count, count)
            ok = (jnp.abs(qr[flat, :] - kr[b]) <= RADIUS) & (jnp.abs(qc[flat, :] - kc[b]) <= RADIUS)
            bias = jnp.where(ok, 0.0, -1e30)
            q8 = qkv_ref[rows, :, pl.ds(at, lanes)].reshape(count, lanes) * jnp.bfloat16(HDIM ** -0.5)
            g = g_ref[rows, :, pl.ds(at, lanes)].reshape(count, lanes)
            kb = ext[keys, :, pl.ds(at, lanes)].reshape(tall * slots, lanes)
            vb = ext[keys, :, pl.ds(at_v, lanes)].reshape(tall * slots, lanes)
            dqs, dks, dvs = [], [], []
            for h in range(2):
                part = slice(h * HDIM, (h + 1) * HDIM)
                qh, kh, vh, gh = q8[:, part], kb[:, part], vb[:, part], g[:, part]
                s = dot(qh, kh, nt) + bias
                ex = jnp.exp(s - jnp.max(s, axis=1, keepdims=True))
                p = ex * (1.0 / jnp.sum(ex, axis=1, keepdims=True))
                pb = p.astype(jnp.bfloat16)
                att = jnp.dot(pb, vh, preferred_element_type=jnp.float32)
                delta = jnp.sum(gh.astype(jnp.float32) * att, axis=1, keepdims=True)
                dp = dot(gh, vh, nt)
                ds = (p * (dp - delta)).astype(jnp.bfloat16)
                dqs.append(jnp.dot(ds, kh, preferred_element_type=jnp.float32) * (HDIM ** -0.5))
                dks.append(dot(ds, qh, tn))
                dvs.append(dot(pb, gh, tn))
            dq = jnp.concatenate(dqs, axis=1)
            if more is not None:
                more.turned[pl.ds(at, lanes), pl.ds(b * count, count)] = dq.T.astype(out_ref.dtype)
            out_ref[rows, :, pl.ds(at, lanes)] = dq.astype(out_ref.dtype).reshape(step, wide, lanes)
            both = jnp.concatenate(dks + dvs, axis=1).reshape(tall, slots, 2 * lanes)
            acc[grp, keys] += both
        for i, d in enumerate(DIRS):

            @pl.when(exists(d))
            def _():
                backward(i, grp).start()

        return carry

    lax.fori_loop(0, groups, one_group, 0)
    if more is not None:
        more.early()

    def collect(grp, carry):
        for i, d in enumerate(DIRS):
            mine = own_pairs(d[0])
            here = pl.ds(half + mine.start, mine.size)

            @pl.when(exists(d))
            def _():
                backward_in(i, grp).wait_recv()
                if d[1] == 0:
                    acc[grp, here, pl.ds(0, wide)] += back[i][grp]
                else:
                    for r in range(2):
                        to = r * cols + (0 if d[1] < 0 else cols - side // 2)
                        acc[grp, here, pl.ds(to, side // 2)] += back[i][grp, :, pl.ds(r * side // 2, side // 2)]

        for j in range(2):
            to = pl.multiple_of(grp * lanes + (j + 1) * width, lanes)
            own = acc[grp, pl.ds(half, pairs), pl.ds(0, wide), pl.ds(j * lanes, lanes)]
            if more is not None:
                more.turned[pl.ds(to, lanes), :] = own.reshape(pairs * wide, lanes).T.astype(out_ref.dtype)
            out_ref[:, :, pl.ds(to, lanes)] = own.astype(out_ref.dtype)
        return carry

    lax.fori_loop(0, groups, collect, 0)
    if more is not None:
        more.finish()

    for i, d in enumerate(DIRS):

        @pl.when(exists(d))
        def _():
            for grp in range(groups):
                for j in range(2):
                    forward(i, grp, j).wait_send()
                backward(i, grp).wait_send()


def halo_attention(qkv, first, last, g, qr, qc, kr, kc, slots, nn, ne):
    pairs, wide, total = qkv.shape
    half, width = RADIUS // 2, total // 3
    groups, side = width // 128, (slots - wide) // 2
    tall = pairs + 2 * half
    dma = pltpu.SemaphoreType.DMA
    vm = pl.BlockSpec(memory_space=pltpu.VMEM)
    back = [
        pltpu.VMEM((groups, half if dn else pairs, side if de else wide, 256), jnp.float32)
        for dn, de in DIRS
    ]
    return pl.pallas_call(
        functools.partial(halo_attention_kernel, nn, ne, None),
        out_shape=jax.ShapeDtypeStruct(qkv.shape, jnp.bfloat16),
        in_specs=[vm] * 8,
        out_specs=vm,
        scratch_shapes=[
            pltpu.VMEM((tall, slots, 2 * width), jnp.bfloat16),
            pltpu.VMEM((groups, tall, slots, 256), jnp.float32),
        ]
        + back
        + [dma((8, groups, 2)), dma((8, groups, 2)), dma((8, groups)), dma((8, groups))],
        compiler_params=pltpu.CompilerParams(
            collective_id=2, has_side_effects=True, vmem_limit_bytes=44 << 20
        ),
        cost_estimate=pl.CostEstimate(
            flops=14 * pairs * wide * tall * slots * width,
            bytes_accessed=4 << 20,
            transcendentals=pairs * wide * tall * slots * HEADS,
        ),
    )(qr, qc, kr, kc, qkv, first, last, g)


CH = 128


def weight_kernel(
    nn, ne, base, tok_ref, dq_ref, out_ref, recv, part, slots,
    a_send, a_recv, r_send, r_recv, z_send, z_recv, p_send, p_recv, f_send, f_recv,
):
    e, n = lax.axis_index("ew"), lax.axis_index("ns")
    share = recv.shape[1]
    count = tok_ref.shape[0] // nn
    chunks = part.shape[0]
    owner = [min((c + 1) // 2, ne - 1) for c in range(chunks)]
    slot_of = [sum(1 for d in range(c) if owner[d] == owner[c]) for c in range(chunks)]
    core = lax.rem(n, 2)
    sibling = n + 1 - 2 * core

    def rows_of(d):
        return pl.ds(pl.multiple_of(base + d * share, 16), share)

    def at(d, m):
        return (d, m)

    def exchange(k):
        to = lax.rem(n + k, nn)
        return pltpu.make_async_remote_copy(
            src_ref=dq_ref.at[rows_of(to)], dst_ref=recv.at[n],
            send_sem=a_send.at[k], recv_sem=a_recv.at[n],
            device_id=at(e, to), device_id_type=MESH,
        )

    def arrived(k):
        src = lax.rem(n + nn - k, nn)
        return pltpu.make_async_remote_copy(
            src_ref=recv.at[src], dst_ref=recv.at[src],
            send_sem=a_send.at[k], recv_sem=a_recv.at[src],
            device_id=at(e, src), device_id_type=MESH,
        )

    for k in range(1, nn):
        exchange(k).start()
    recv[n] = dq_ref[rows_of(n), :]
    yield
    for k in range(1, nn):
        arrived(k).wait_recv()

    def reduce_copy(c, src):
        return pltpu.make_async_remote_copy(
            src_ref=part.at[c], dst_ref=slots.at[slot_of[c], src],
            send_sem=r_send.at[c], recv_sem=r_recv.at[slot_of[c], src],
            device_id=at(owner[c], n), device_id_type=MESH,
        )

    order = [c for c in range(chunks)]
    for c in order:
        total = jnp.zeros((share, CH), jnp.float32)
        for s in range(nn):
            total += jnp.dot(
                recv[s], tok_ref[s * count : (s + 1) * count, c * CH : (c + 1) * CH],
                preferred_element_type=jnp.float32,
            )
        part[c] = total

        @pl.when(e != owner[c])
        def _():
            reduce_copy(c, e).start()

    yield

    def spot(c, m):
        return out_ref.at[rows_of(m), c * CH : (c + 1) * CH]

    def column_copy(c, k):
        return pltpu.make_async_remote_copy(
            src_ref=spot(c, n), dst_ref=spot(c, n),
            send_sem=z_send.at[c, k], recv_sem=z_recv.at[c],
            device_id=at(lax.rem(owner[c] + k, ne), n), device_id_type=MESH,
        )

    def plane_copy(c, m, to, sem, k, rsem):
        return pltpu.make_async_remote_copy(
            src_ref=spot(c, m), dst_ref=spot(c, m),
            send_sem=sem.at[c, k], recv_sem=rsem.at[c, m],
            device_id=at(e, to), device_id_type=MESH,
        )

    def peers(k):
        return lax.rem(n + 2 * k, nn)

    def spread(c):
        for k in range(1, nn // 2):
            plane_copy(c, n, peers(k), p_send, k, p_recv).start()
        plane_copy(c, n, sibling, p_send, 0, p_recv).start()

    for c in order:

        @pl.when(e == owner[c])
        def _():
            total = part[c]
            for k in range(1, ne):
                src = (owner[c] + k) % ne
                reduce_copy(c, src).wait_recv()
                total += slots[slot_of[c], src]
            out_ref[rows_of(n), c * CH : (c + 1) * CH] = total.astype(jnp.bfloat16)
            for k in range(1, ne):
                column_copy(c, k).start()
            spread(c)

    yield
    for c in order:

        @pl.when(e != owner[c])
        def _():
            column_copy(c, 1).wait_recv()
            spread(c)

    yield
    for c in order:
        for k in range(1, nn // 2):
            m = peers(k)
            plane_copy(c, m, sibling, p_send, 0, p_recv).wait_recv()
            plane_copy(c, m, sibling, f_send, k, f_recv).start()

    yield
    for c in order:
        plane_copy(c, sibling, sibling, p_send, 0, p_recv).wait_recv()
        for k in range(1, nn // 2):
            m = lax.rem(sibling + 2 * k, nn)
            plane_copy(c, m, sibling, f_send, k, f_recv).wait_recv()

    for k in range(1, nn):
        exchange(k).wait_send()
    for c in order:

        @pl.when(e != owner[c])
        def _():
            reduce_copy(c, e).wait_send()

        @pl.when(e == owner[c])
        def _():
            for k in range(1, ne):
                column_copy(c, k).wait_send()

        for k in range(nn // 2):
            plane_copy(c, n, sibling, p_send, k, p_recv).wait_send()
        for k in range(1, nn // 2):
            plane_copy(c, n, sibling, f_send, k, f_recv).wait_send()


class More:
    def __init__(self, nn, ne, tok, w, gt, gw, everything, dqkv, turned, sems, rest):
        self.nn, self.ne, self.tok, self.w, self.gt, self.gw = nn, ne, tok, w, gt, gw
        self.everything, self.dqkv, self.turned, self.rest = everything, dqkv, turned, rest
        self.t_send, self.t_recv, self.u_send, self.u_recv = sems
        self.e, self.n = lax.axis_index("ew"), lax.axis_index("ns")
        self.sibling = self.n + 1 - 2 * lax.rem(self.n, 2)
        self.count = tok.shape[0]

    def block(self, m):
        return pl.ds(pl.multiple_of(m * self.count, self.count), self.count)

    def peer(self, k, base=None):
        return self.sibling if k == 0 else lax.rem((self.n if base is None else base) + 2 * k, self.nn)

    def send(self, k):
        return pltpu.make_async_remote_copy(
            src_ref=self.tok, dst_ref=self.everything.at[self.block(self.n)],
            send_sem=self.t_send.at[k], recv_sem=self.t_recv.at[self.n],
            device_id=(self.e, self.peer(k)), device_id_type=MESH,
        )

    def pass_on(self, k, m, recv):
        return pltpu.make_async_remote_copy(
            src_ref=self.everything.at[self.block(m)], dst_ref=self.everything.at[self.block(m)],
            send_sem=self.u_send.at[k], recv_sem=recv.at[m],
            device_id=(self.e, self.sibling), device_id_type=MESH,
        )

    def start(self):
        for k in range(self.nn // 2):
            self.send(k).start()
        self.everything[self.block(self.n), :] = self.tok[...]

    def forward(self):
        for k in range(1, self.nn // 2):
            self.pass_on(k, self.peer(k), self.t_recv).wait_recv()
            self.pass_on(k, self.peer(k), self.u_recv).start()

    def early(self):
        half = len(self.rest) // 2
        width = self.turned.shape[0] // 3
        make = lambda base, rest: weight_kernel(
            self.nn, self.ne, base, self.everything, self.turned, self.gw, *rest
        )
        self.parts = [make(0, self.rest[:half]), make(width, self.rest[half:])]
        next(self.parts[0])
        self.forward()

    def tokens_in(self):
        self.pass_on(0, self.sibling, self.t_recv).wait_recv()
        for k in range(1, self.nn // 2):
            m = lax.rem(self.sibling + 2 * k, self.nn)
            self.pass_on(k, m, self.u_recv).wait_recv()

    def mid(self):
        dq = self.dqkv[...].reshape(self.count, self.dqkv.shape[2])
        for c in range(0, self.w.shape[0], 256):
            self.gt[:, c : c + 256] = lax.dot_general(
                dq, self.w[c : c + 256, :], (((1,), (1,)), ((), ())), preferred_element_type=jnp.float32
            ).astype(jnp.bfloat16)

    def finish(self):
        first, second = self.parts
        next(second)
        self.tokens_in()
        next(first)
        self.mid()
        next(second)
        for _ in range(3):
            next(first)
            next(second)
        next(first, None)
        next(second, None)
        for k in range(self.nn // 2):
            self.send(k).wait_send()
        for k in range(1, self.nn // 2):
            self.pass_on(k, self.peer(k), self.u_recv).wait_send()


def fused_kernel(nn, ne, *refs):
    qr, qc, kr, kc, qkv, first, last, g, tok, w, gt, gw, everything, dqkv, turned = refs[:15]
    sems, scratch, rest = refs[15:19], refs[19:33], refs[33:]
    more = More(nn, ne, tok, w, gt, gw, everything, dqkv, turned, sems, rest)
    halo_attention_kernel(nn, ne, more, qr, qc, kr, kc, qkv, first, last, g, dqkv, *scratch)


def fused(qkv, first, last, g, qr, qc, kr, kc, slots, nn, ne, tok, w):
    pairs, wide, total = qkv.shape
    count, features = tok.shape
    half, width = RADIUS // 2, total // 3
    groups, side = width // 128, (slots - wide) // 2
    tall = pairs + 2 * half
    chunks = features // CH
    dma = pltpu.SemaphoreType.DMA

    def weight_scratch(share):
        return [
            pltpu.VMEM((nn, share, count), jnp.bfloat16),
            pltpu.VMEM((chunks, share, CH), jnp.float32),
            pltpu.VMEM((2, ne, share, CH), jnp.float32),
            dma((nn,)), dma((nn,)),
            dma((chunks,)), dma((2, ne)),
            dma((chunks, ne)), dma((chunks,)),
            dma((chunks, nn // 2)), dma((chunks, nn)),
            dma((chunks, nn // 2)), dma((chunks, nn)),
        ]

    vm = pl.BlockSpec(memory_space=pltpu.VMEM)
    back = [
        pltpu.VMEM((groups, half if dn else pairs, side if de else wide, 256), jnp.float32)
        for dn, de in DIRS
    ]
    return pl.pallas_call(
        functools.partial(fused_kernel, nn, ne),
        out_shape=[
            jax.ShapeDtypeStruct((count, features), jnp.bfloat16),
            jax.ShapeDtypeStruct((total, features), jnp.bfloat16),
        ],
        in_specs=[vm] * 10,
        out_specs=[vm, vm],
        scratch_shapes=[
            pltpu.VMEM((nn * count, features), jnp.bfloat16),
            pltpu.VMEM((pairs, wide, total), jnp.bfloat16),
            pltpu.VMEM((total, count), jnp.bfloat16),
            dma((nn // 2,)), dma((nn,)), dma((nn // 2,)), dma((nn,)),
            pltpu.VMEM((tall, slots, 2 * width), jnp.bfloat16),
            pltpu.VMEM((groups, tall, slots, 256), jnp.float32),
        ]
        + back
        + [
            dma((8, groups, 2)), dma((8, groups, 2)), dma((8, groups)), dma((8, groups)),
        ]
        + weight_scratch(width // nn)
        + weight_scratch(2 * width // nn),
        compiler_params=pltpu.CompilerParams(
            collective_id=1, has_side_effects=True, vmem_limit_bytes=44 << 20
        ),
        cost_estimate=pl.CostEstimate(
            flops=14 * pairs * wide * tall * slots * width + 4 * count * features * total,
            bytes_accessed=8 << 20,
            transcendentals=pairs * wide * tall * slots * HEADS,
        ),
    )(qr, qc, kr, kc, qkv, first, last, g, tok, w)


def local(tokens, w_qkv, grad_out):
    tile_rows, tile_cols, features = tokens.shape
    nn, ne = lax.axis_size("ns"), lax.axis_size("ew")
    width = w_qkv.shape[1] // 3
    count = tile_rows * tile_cols
    flat_tokens = tokens.reshape(count, features)
    paired = nn == 8 and ne == 4
    projected = jnp.dot(flat_tokens, w_qkv, preferred_element_type=jnp.float32).astype(jnp.bfloat16)
    half, pairs, wide, edge = RADIUS // 2, tile_rows // 2, 2 * tile_cols, 8
    slots = wide + 4 * edge
    qkv = projected.reshape(pairs, wide, 3 * width)
    by_row = projected[:, width:].reshape(tile_rows, tile_cols, 2 * width)
    first = by_row[:, :edge].reshape(pairs, 2 * edge, 2 * width)
    last = by_row[:, tile_cols - edge :].reshape(pairs, 2 * edge, 2 * width)
    nb = 2
    row0 = lax.axis_index("ns") * tile_rows
    col0 = lax.axis_index("ew") * tile_cols
    qi = jnp.arange(count, dtype=jnp.int32)
    qr = (row0 + qi // tile_cols)[:, None]
    qc = (col0 + qi % tile_cols)[:, None]
    slot = np.arange(slots)
    in_side = np.maximum(slot - wide, 0)
    slot_row = np.where(slot < wide, slot // tile_cols, (in_side % (2 * edge)) // edge)
    slot_col = np.where(
        slot < wide,
        slot % tile_cols,
        np.where(in_side < 2 * edge, tile_cols + in_side % edge, in_side % edge - edge),
    )
    ext_row = (2 * np.arange(pairs + 2 * half)[:, None] - RADIUS + slot_row[None]).astype(np.int32)
    ext_col = np.broadcast_to(slot_col[None], ext_row.shape).astype(np.int32)
    kr, kc = row0 + ext_row, col0 + ext_col
    inside = (kr >= 0) & (kr < nn * tile_rows) & (kc >= 0) & (kc < ne * tile_cols)
    kr = jnp.where(inside, kr, -1000)
    per = pairs // nb
    pick = lambda a: jnp.stack([a[b * per : b * per + per + 2 * half].reshape(1, -1) for b in range(nb)])
    halo_args = (
        qkv, first, last, grad_out.reshape(pairs, wide, width), qr, qc, pick(kr), pick(kc), slots, nn, ne
    )
    if paired:
        grad_tokens, grad_w_t = fused(*halo_args, flat_tokens, w_qkv)
        return (grad_tokens.reshape(tokens.shape), grad_w_t.T)
    dqkv = halo_attention(*halo_args).reshape(count, 3 * width)
    grad_tokens = (
        jnp.dot(dqkv, w_qkv.T, preferred_element_type=jnp.float32)
        .astype(jnp.bfloat16)
        .reshape(tile_rows, tile_cols, features)
    )
    weight_part = lax.dot_general(
        flat_tokens, dqkv, (((0,), (0,)), ((), ())), preferred_element_type=jnp.float32
    )
    grad_w = lax.psum(weight_part, ("ew", "ns")).astype(jnp.bfloat16)
    return (grad_tokens, grad_w)


def solution(mesh):
    in_specs = (P("ns", "ew", None), P(), P("ns", "ew", None))
    out_specs = (P("ns", "ew", None), P())
    return jax.shard_map(local, mesh=mesh, in_specs=in_specs, out_specs=out_specs, check_vma=False)
```

```python
import functools

import jax
import jax.numpy as jnp
import numpy as np
from jax import lax
from jax.experimental import pallas as pl
from jax.experimental.pallas import tpu as pltpu
from jax.sharding import PartitionSpec as P

HEADS = 6
HDIM = 64
RADIUS = 6
MESH = pl.DeviceIdType.MESH


DIRS = [(dn, de) for dn in (-1, 0, 1) for de in (-1, 0, 1) if (dn, de) != (0, 0)]


def halo_attention_kernel(
    nn, ne, more, qr, qc, kr, kc, qkv_ref, first_ref, last_ref, g_ref, out_ref, ext, acc, *rest
):
    back = rest[:8]
    f_send, f_recv, b_send, b_recv = rest[8:]
    e, n = lax.axis_index("ew"), lax.axis_index("ns")
    pairs, wide, total = qkv_ref.shape
    width = total // 3
    half = RADIUS // 2
    groups, lanes = width // 128, 128
    slots = ext.shape[1]
    side = (slots - wide) // 2
    nb = kr.shape[0]
    step = pairs // nb
    tall = step + 2 * half
    cols = wide // 2

    def exists(d):
        dn, de = d
        return (n + dn >= 0) & (n + dn < nn) & (e + de >= 0) & (e + de < ne)

    def own_pairs(dn):
        return {-1: pl.ds(0, half), 0: pl.ds(0, pairs), 1: pl.ds(pairs - half, half)}[dn]

    def region(d):
        rows = {-1: pl.ds(0, half), 0: pl.ds(half, pairs), 1: pl.ds(half + pairs, half)}[d[0]]
        place = {0: pl.ds(0, wide), 1: pl.ds(wide, side), -1: pl.ds(wide + side, side)}[d[1]]
        return rows, place

    def opposite(i):
        return DIRS.index((-DIRS[i][0], -DIRS[i][1]))

    def lane(grp, j, start=0):
        return pl.ds(pl.multiple_of(start + j * width + grp * lanes, lanes), lanes)

    def forward(i, grp, j):
        dn, de = DIRS[i]
        rows = own_pairs(dn)
        if de == 0:
            src = qkv_ref.at[rows, :, lane(grp, j, width)]
        else:
            src = (first_ref if de < 0 else last_ref).at[rows, :, lane(grp, j)]
        there = opposite(i)
        a, b = region(DIRS[there])
        return pltpu.make_async_remote_copy(
            src_ref=src, dst_ref=ext.at[a, b, lane(grp, j)],
            send_sem=f_send.at[i, grp, j], recv_sem=f_recv.at[there, grp, j],
            device_id=(e + de, n + dn), device_id_type=MESH,
        )

    def forward_in(i, grp, j):
        a, b = region(DIRS[i])
        here = ext.at[a, b, lane(grp, j)]
        return pltpu.make_async_remote_copy(
            src_ref=here, dst_ref=here, send_sem=f_send.at[i, grp, j], recv_sem=f_recv.at[i, grp, j],
            device_id=(e + DIRS[i][1], n + DIRS[i][0]), device_id_type=MESH,
        )

    def strips_in(grp):
        for i, d in enumerate(DIRS):

            @pl.when(exists(d))
            def _():
                for j in range(2):
                    forward_in(i, grp, j).wait_recv()

    def backward(i, grp):
        a, b = region(DIRS[i])
        there = opposite(i)
        return pltpu.make_async_remote_copy(
            src_ref=acc.at[grp, a, b], dst_ref=back[there].at[grp],
            send_sem=b_send.at[i, grp], recv_sem=b_recv.at[there, grp],
            device_id=(e + DIRS[i][1], n + DIRS[i][0]), device_id_type=MESH,
        )

    def backward_in(i, grp):
        return pltpu.make_async_remote_copy(
            src_ref=back[i].at[grp], dst_ref=back[i].at[grp],
            send_sem=b_send.at[i, grp], recv_sem=b_recv.at[i, grp],
            device_id=(e + DIRS[i][1], n + DIRS[i][0]), device_id_type=MESH,
        )

    near = DIRS
    barrier = pltpu.get_barrier_semaphore()
    if more is not None:
        near = [d for d in DIRS if d[0] and d[1]]
        for k in range(1, nn):
            pl.semaphore_signal(barrier, inc=1, device_id=(e, lax.rem(n + k, nn)), device_id_type=MESH)
        for k in range(1, ne):
            pl.semaphore_signal(barrier, inc=1, device_id=(lax.rem(e + k, ne), n), device_id_type=MESH)
    for d in near:

        @pl.when(exists(d))
        def _():
            pl.semaphore_signal(barrier, inc=1, device_id=(e + d[1], n + d[0]), device_id_type=MESH)

    others = nn - 1 + ne - 1 if more is not None else 0
    pl.semaphore_wait(barrier, others + sum(exists(d).astype(jnp.int32) for d in near))

    for grp in range(groups):
        for i, d in enumerate(DIRS):

            @pl.when(exists(d))
            def _():
                for j in range(2):
                    forward(i, grp, j).start()

    if more is not None:
        more.start()
    ext[pl.ds(half, pairs), pl.ds(0, wide), :] = qkv_ref[:, :, pl.ds(width, 2 * width)]
    acc[...] = jnp.zeros_like(acc)
    for i, d in enumerate(DIRS):
        a, b = region(d)

        @pl.when(jnp.logical_not(exists(d)))
        def _():
            ext[a, b, :] = jnp.zeros((a.size, b.size, 2 * width), ext.dtype)

    strips_in(0)
    nt = (((1,), (1,)), ((), ()))
    tn = (((0,), (0,)), ((), ()))
    dot = functools.partial(lax.dot_general, preferred_element_type=jnp.float32)
    count = step * wide

    def one_group(grp, carry):
        @pl.when(grp > 0)
        def _():
            strips_in(grp)

        at = pl.multiple_of(grp * lanes, lanes)
        at_v = pl.multiple_of(grp * lanes + width, lanes)
        for b in range(nb):
            rows = pl.ds(b * step, step)
            keys = pl.ds(b * step, tall)
            flat = pl.ds(b * count, count)
            ok = (jnp.abs(qr[flat, :] - kr[b]) <= RADIUS) & (jnp.abs(qc[flat, :] - kc[b]) <= RADIUS)
            bias = jnp.where(ok, 0.0, -1e30)
            q8 = qkv_ref[rows, :, pl.ds(at, lanes)].reshape(count, lanes) * jnp.bfloat16(HDIM ** -0.5)
            g = g_ref[rows, :, pl.ds(at, lanes)].reshape(count, lanes)
            kb = ext[keys, :, pl.ds(at, lanes)].reshape(tall * slots, lanes)
            vb = ext[keys, :, pl.ds(at_v, lanes)].reshape(tall * slots, lanes)
            dqs, dks, dvs = [], [], []
            for h in range(2):
                part = slice(h * HDIM, (h + 1) * HDIM)
                qh, kh, vh, gh = q8[:, part], kb[:, part], vb[:, part], g[:, part]
                s = dot(qh, kh, nt) + bias
                ex = jnp.exp(s - jnp.max(s, axis=1, keepdims=True))
                p = ex * (1.0 / jnp.sum(ex, axis=1, keepdims=True))
                pb = p.astype(jnp.bfloat16)
                att = jnp.dot(pb, vh, preferred_element_type=jnp.float32)
                delta = jnp.sum(gh.astype(jnp.float32) * att, axis=1, keepdims=True)
                dp = dot(gh, vh, nt)
                ds = (p * (dp - delta)).astype(jnp.bfloat16)
                dqs.append(jnp.dot(ds, kh, preferred_element_type=jnp.float32) * (HDIM ** -0.5))
                dks.append(dot(ds, qh, tn))
                dvs.append(dot(pb, gh, tn))
            dq = jnp.concatenate(dqs, axis=1)
            if more is not None:
                more.turned[pl.ds(at, lanes), pl.ds(b * count, count)] = dq.T.astype(out_ref.dtype)
            out_ref[rows, :, pl.ds(at, lanes)] = dq.astype(out_ref.dtype).reshape(step, wide, lanes)
            both = jnp.concatenate(dks + dvs, axis=1).reshape(tall, slots, 2 * lanes)
            acc[grp, keys] += both
        for i, d in enumerate(DIRS):

            @pl.when(exists(d))
            def _():
                backward(i, grp).start()

        return carry

    lax.fori_loop(0, groups, one_group, 0)
    if more is not None:
        more.early()

    def collect(grp, carry):
        for i, d in enumerate(DIRS):
            mine = own_pairs(d[0])
            here = pl.ds(half + mine.start, mine.size)

            @pl.when(exists(d))
            def _():
                backward_in(i, grp).wait_recv()
                if d[1] == 0:
                    acc[grp, here, pl.ds(0, wide)] += back[i][grp]
                else:
                    for r in range(2):
                        to = r * cols + (0 if d[1] < 0 else cols - side // 2)
                        acc[grp, here, pl.ds(to, side // 2)] += back[i][grp, :, pl.ds(r * side // 2, side // 2)]

        for j in range(2):
            to = pl.multiple_of(grp * lanes + (j + 1) * width, lanes)
            own = acc[grp, pl.ds(half, pairs), pl.ds(0, wide), pl.ds(j * lanes, lanes)]
            if more is not None:
                more.turned[pl.ds(to, lanes), :] = own.reshape(pairs * wide, lanes).T.astype(out_ref.dtype)
            out_ref[:, :, pl.ds(to, lanes)] = own.astype(out_ref.dtype)
        return carry

    lax.fori_loop(0, groups, collect, 0)
    if more is not None:
        more.finish()

    for i, d in enumerate(DIRS):

        @pl.when(exists(d))
        def _():
            for grp in range(groups):
                for j in range(2):
                    forward(i, grp, j).wait_send()
                backward(i, grp).wait_send()


def halo_attention(qkv, first, last, g, qr, qc, kr, kc, slots, nn, ne):
    pairs, wide, total = qkv.shape
    half, width = RADIUS // 2, total // 3
    groups, side = width // 128, (slots - wide) // 2
    tall = pairs + 2 * half
    dma = pltpu.SemaphoreType.DMA
    vm = pl.BlockSpec(memory_space=pltpu.VMEM)
    back = [
        pltpu.VMEM((groups, half if dn else pairs, side if de else wide, 256), jnp.float32)
        for dn, de in DIRS
    ]
    return pl.pallas_call(
        functools.partial(halo_attention_kernel, nn, ne, None),
        out_shape=jax.ShapeDtypeStruct(qkv.shape, jnp.bfloat16),
        in_specs=[vm] * 8,
        out_specs=vm,
        scratch_shapes=[
            pltpu.VMEM((tall, slots, 2 * width), jnp.bfloat16),
            pltpu.VMEM((groups, tall, slots, 256), jnp.float32),
        ]
        + back
        + [dma((8, groups, 2)), dma((8, groups, 2)), dma((8, groups)), dma((8, groups))],
        compiler_params=pltpu.CompilerParams(
            collective_id=2, has_side_effects=True, vmem_limit_bytes=44 << 20
        ),
        cost_estimate=pl.CostEstimate(
            flops=14 * pairs * wide * tall * slots * width,
            bytes_accessed=4 << 20,
            transcendentals=pairs * wide * tall * slots * HEADS,
        ),
    )(qr, qc, kr, kc, qkv, first, last, g)


CH = 128


def weight_kernel(
    nn, ne, base, tok_ref, dq_ref, out_ref, recv, part, slots,
    a_send, a_recv, r_send, r_recv, z_send, z_recv, p_send, p_recv, f_send, f_recv,
):
    e, n = lax.axis_index("ew"), lax.axis_index("ns")
    share = recv.shape[1]
    count = tok_ref.shape[0] // nn
    chunks = part.shape[0]
    owner = [min((c + 1) // 2, ne - 1) for c in range(chunks)]
    slot_of = [sum(1 for d in range(c) if owner[d] == owner[c]) for c in range(chunks)]
    core = lax.rem(n, 2)
    sibling = n + 1 - 2 * core

    def rows_of(d):
        return pl.ds(pl.multiple_of(base + d * share, 16), share)

    def at(d, m):
        return (d, m)

    def exchange(k):
        to = lax.rem(n + k, nn)
        return pltpu.make_async_remote_copy(
            src_ref=dq_ref.at[rows_of(to)], dst_ref=recv.at[n],
            send_sem=a_send.at[k], recv_sem=a_recv.at[n],
            device_id=at(e, to), device_id_type=MESH,
        )

    def arrived(k):
        src = lax.rem(n + nn - k, nn)
        return pltpu.make_async_remote_copy(
            src_ref=recv.at[src], dst_ref=recv.at[src],
            send_sem=a_send.at[k], recv_sem=a_recv.at[src],
            device_id=at(e, src), device_id_type=MESH,
        )

    for k in range(1, nn):
        exchange(k).start()
    recv[n] = dq_ref[rows_of(n), :]
    yield
    for k in range(1, nn):
        arrived(k).wait_recv()

    def reduce_copy(c, src):
        return pltpu.make_async_remote_copy(
            src_ref=part.at[c], dst_ref=slots.at[slot_of[c], src],
            send_sem=r_send.at[c], recv_sem=r_recv.at[slot_of[c], src],
            device_id=at(owner[c], n), device_id_type=MESH,
        )

    order = [c for c in range(chunks)]
    for c in order:
        total = jnp.zeros((share, CH), jnp.float32)
        for s in range(nn):
            total += jnp.dot(
                recv[s], tok_ref[s * count : (s + 1) * count, c * CH : (c + 1) * CH],
                preferred_element_type=jnp.float32,
            )
        part[c] = total

        @pl.when(e != owner[c])
        def _():
            reduce_copy(c, e).start()

    yield

    def spot(c, m):
        return out_ref.at[rows_of(m), c * CH : (c + 1) * CH]

    def column_copy(c, k):
        return pltpu.make_async_remote_copy(
            src_ref=spot(c, n), dst_ref=spot(c, n),
            send_sem=z_send.at[c, k], recv_sem=z_recv.at[c],
            device_id=at(lax.rem(owner[c] + k, ne), n), device_id_type=MESH,
        )

    def plane_copy(c, m, to, sem, k, rsem):
        return pltpu.make_async_remote_copy(
            src_ref=spot(c, m), dst_ref=spot(c, m),
            send_sem=sem.at[c, k], recv_sem=rsem.at[c, m],
            device_id=at(e, to), device_id_type=MESH,
        )

    def peers(k):
        return lax.rem(n + 2 * k, nn)

    def spread(c):
        for k in range(1, nn // 2):
            plane_copy(c, n, peers(k), p_send, k, p_recv).start()
        plane_copy(c, n, sibling, p_send, 0, p_recv).start()

    for c in order:

        @pl.when(e == owner[c])
        def _():
            total = part[c]
            for k in range(1, ne):
                src = (owner[c] + k) % ne
                reduce_copy(c, src).wait_recv()
                total += slots[slot_of[c], src]
            out_ref[rows_of(n), c * CH : (c + 1) * CH] = total.astype(jnp.bfloat16)
            for k in range(1, ne):
                column_copy(c, k).start()
            spread(c)

    yield
    for c in order:

        @pl.when(e != owner[c])
        def _():
            column_copy(c, 1).wait_recv()
            spread(c)

    yield
    for c in order:
        for k in range(1, nn // 2):
            m = peers(k)
            plane_copy(c, m, sibling, p_send, 0, p_recv).wait_recv()
            plane_copy(c, m, sibling, f_send, k, f_recv).start()

    yield
    for c in order:
        plane_copy(c, sibling, sibling, p_send, 0, p_recv).wait_recv()
        for k in range(1, nn // 2):
            m = lax.rem(sibling + 2 * k, nn)
            plane_copy(c, m, sibling, f_send, k, f_recv).wait_recv()

    for k in range(1, nn):
        exchange(k).wait_send()
    for c in order:

        @pl.when(e != owner[c])
        def _():
            reduce_copy(c, e).wait_send()

        @pl.when(e == owner[c])
        def _():
            for k in range(1, ne):
                column_copy(c, k).wait_send()

        for k in range(nn // 2):
            plane_copy(c, n, sibling, p_send, k, p_recv).wait_send()
        for k in range(1, nn // 2):
            plane_copy(c, n, sibling, f_send, k, f_recv).wait_send()


class More:
    def __init__(self, nn, ne, tok, w, gt, gw, everything, dqkv, turned, sems, rest):
        self.nn, self.ne, self.tok, self.w, self.gt, self.gw = nn, ne, tok, w, gt, gw
        self.everything, self.dqkv, self.turned, self.rest = everything, dqkv, turned, rest
        self.t_send, self.t_recv, self.u_send, self.u_recv = sems
        self.e, self.n = lax.axis_index("ew"), lax.axis_index("ns")
        self.sibling = self.n + 1 - 2 * lax.rem(self.n, 2)
        self.count = tok.shape[0]

    def block(self, m):
        return pl.ds(pl.multiple_of(m * self.count, self.count), self.count)

    def peer(self, k, base=None):
        return self.sibling if k == 0 else lax.rem((self.n if base is None else base) + 2 * k, self.nn)

    def send(self, k):
        return pltpu.make_async_remote_copy(
            src_ref=self.tok, dst_ref=self.everything.at[self.block(self.n)],
            send_sem=self.t_send.at[k], recv_sem=self.t_recv.at[self.n],
            device_id=(self.e, self.peer(k)), device_id_type=MESH,
        )

    def pass_on(self, k, m, recv):
        return pltpu.make_async_remote_copy(
            src_ref=self.everything.at[self.block(m)], dst_ref=self.everything.at[self.block(m)],
            send_sem=self.u_send.at[k], recv_sem=recv.at[m],
            device_id=(self.e, self.sibling), device_id_type=MESH,
        )

    def start(self):
        for k in range(self.nn // 2):
            self.send(k).start()
        self.everything[self.block(self.n), :] = self.tok[...]

    def forward(self):
        for k in range(1, self.nn // 2):
            self.pass_on(k, self.peer(k), self.t_recv).wait_recv()
            self.pass_on(k, self.peer(k), self.u_recv).start()

    def early(self):
        half = len(self.rest) // 2
        width = self.turned.shape[0] // 3
        make = lambda base, rest: weight_kernel(
            self.nn, self.ne, base, self.everything, self.turned, self.gw, *rest
        )
        self.parts = [make(0, self.rest[:half]), make(width, self.rest[half:])]
        next(self.parts[0])
        self.forward()

    def tokens_in(self):
        self.pass_on(0, self.sibling, self.t_recv).wait_recv()
        for k in range(1, self.nn // 2):
            m = lax.rem(self.sibling + 2 * k, self.nn)
            self.pass_on(k, m, self.u_recv).wait_recv()

    def mid(self):
        dq = self.dqkv[...].reshape(self.count, self.dqkv.shape[2])
        for c in range(0, self.w.shape[0], 256):
            self.gt[:, c : c + 256] = lax.dot_general(
                dq, self.w[c : c + 256, :], (((1,), (1,)), ((), ())), preferred_element_type=jnp.float32
            ).astype(jnp.bfloat16)

    def finish(self):
        first, second = self.parts
        next(second)
        self.tokens_in()
        next(first)
        self.mid()
        next(second)
        for _ in range(3):
            next(first)
            next(second)
        next(first, None)
        next(second, None)
        for k in range(self.nn // 2):
            self.send(k).wait_send()
        for k in range(1, self.nn // 2):
            self.pass_on(k, self.peer(k), self.u_recv).wait_send()


def fused_kernel(nn, ne, *refs):
    qr, qc, kr, kc, qkv, first, last, g, tok, w, gt, gw, everything, dqkv, turned = refs[:15]
    sems, scratch, rest = refs[15:19], refs[19:33], refs[33:]
    more = More(nn, ne, tok, w, gt, gw, everything, dqkv, turned, sems, rest)
    halo_attention_kernel(nn, ne, more, qr, qc, kr, kc, qkv, first, last, g, dqkv, *scratch)


def fused(qkv, first, last, g, qr, qc, kr, kc, slots, nn, ne, tok, w):
    pairs, wide, total = qkv.shape
    count, features = tok.shape
    half, width = RADIUS // 2, total // 3
    groups, side = width // 128, (slots - wide) // 2
    tall = pairs + 2 * half
    chunks = features // CH
    dma = pltpu.SemaphoreType.DMA

    def weight_scratch(share):
        return [
            pltpu.VMEM((nn, share, count), jnp.bfloat16),
            pltpu.VMEM((chunks, share, CH), jnp.float32),
            pltpu.VMEM((2, ne, share, CH), jnp.float32),
            dma((nn,)), dma((nn,)),
            dma((chunks,)), dma((2, ne)),
            dma((chunks, ne)), dma((chunks,)),
            dma((chunks, nn // 2)), dma((chunks, nn)),
            dma((chunks, nn // 2)), dma((chunks, nn)),
        ]

    vm = pl.BlockSpec(memory_space=pltpu.VMEM)
    back = [
        pltpu.VMEM((groups, half if dn else pairs, side if de else wide, 256), jnp.float32)
        for dn, de in DIRS
    ]
    return pl.pallas_call(
        functools.partial(fused_kernel, nn, ne),
        out_shape=[
            jax.ShapeDtypeStruct((count, features), jnp.bfloat16),
            jax.ShapeDtypeStruct((total, features), jnp.bfloat16),
        ],
        in_specs=[vm] * 10,
        out_specs=[vm, vm],
        scratch_shapes=[
            pltpu.VMEM((nn * count, features), jnp.bfloat16),
            pltpu.VMEM((pairs, wide, total), jnp.bfloat16),
            pltpu.VMEM((total, count), jnp.bfloat16),
            dma((nn // 2,)), dma((nn,)), dma((nn // 2,)), dma((nn,)),
            pltpu.VMEM((tall, slots, 2 * width), jnp.bfloat16),
            pltpu.VMEM((groups, tall, slots, 256), jnp.float32),
        ]
        + back
        + [
            dma((8, groups, 2)), dma((8, groups, 2)), dma((8, groups)), dma((8, groups)),
        ]
        + weight_scratch(width // nn)
        + weight_scratch(2 * width // nn),
        compiler_params=pltpu.CompilerParams(
            collective_id=1, has_side_effects=True, vmem_limit_bytes=44 << 20
        ),
        cost_estimate=pl.CostEstimate(
            flops=14 * pairs * wide * tall * slots * width + 4 * count * features * total,
            bytes_accessed=8 << 20,
            transcendentals=pairs * wide * tall * slots * HEADS,
        ),
    )(qr, qc, kr, kc, qkv, first, last, g, tok, w)


def local(tokens, w_qkv, grad_out):
    tile_rows, tile_cols, features = tokens.shape
    nn, ne = lax.axis_size("ns"), lax.axis_size("ew")
    width = w_qkv.shape[1] // 3
    count = tile_rows * tile_cols
    flat_tokens = tokens.reshape(count, features)
    paired = nn == 8 and ne == 4
    projected = jnp.dot(flat_tokens, w_qkv, preferred_element_type=jnp.float32).astype(jnp.bfloat16)
    half, pairs, wide, edge = RADIUS // 2, tile_rows // 2, 2 * tile_cols, 8
    slots = wide + 4 * edge
    qkv = projected.reshape(pairs, wide, 3 * width)
    by_row = projected[:, width:].reshape(tile_rows, tile_cols, 2 * width)
    first = by_row[:, :edge].reshape(pairs, 2 * edge, 2 * width)
    last = by_row[:, tile_cols - edge :].reshape(pairs, 2 * edge, 2 * width)
    nb = 2
    row0 = lax.axis_index("ns") * tile_rows
    col0 = lax.axis_index("ew") * tile_cols
    qi = jnp.arange(count, dtype=jnp.int32)
    qr = (row0 + qi // tile_cols)[:, None]
    qc = (col0 + qi % tile_cols)[:, None]
    slot = np.arange(slots)
    in_side = np.maximum(slot - wide, 0)
    slot_row = np.where(slot < wide, slot // tile_cols, (in_side % (2 * edge)) // edge)
    slot_col = np.where(
        slot < wide,
        slot % tile_cols,
        np.where(in_side < 2 * edge, tile_cols + in_side % edge, in_side % edge - edge),
    )
    ext_row = (2 * np.arange(pairs + 2 * half)[:, None] - RADIUS + slot_row[None]).astype(np.int32)
    ext_col = np.broadcast_to(slot_col[None], ext_row.shape).astype(np.int32)
    kr, kc = row0 + ext_row, col0 + ext_col
    inside = (kr >= 0) & (kr < nn * tile_rows) & (kc >= 0) & (kc < ne * tile_cols)
    kr = jnp.where(inside, kr, -1000)
    per = pairs // nb
    pick = lambda a: jnp.stack([a[b * per : b * per + per + 2 * half].reshape(1, -1) for b in range(nb)])
    halo_args = (
        qkv, first, last, grad_out.reshape(pairs, wide, width), qr, qc, pick(kr), pick(kc), slots, nn, ne
    )
    if paired:
        grad_tokens, grad_w_t = fused(*halo_args, flat_tokens, w_qkv)
        return (grad_tokens.reshape(tokens.shape), grad_w_t.T)
    dqkv = halo_attention(*halo_args).reshape(count, 3 * width)
    grad_tokens = (
        jnp.dot(dqkv, w_qkv.T, preferred_element_type=jnp.float32)
        .astype(jnp.bfloat16)
        .reshape(tile_rows, tile_cols, features)
    )
    weight_part = lax.dot_general(
        flat_tokens, dqkv, (((0,), (0,)), ((), ())), preferred_element_type=jnp.float32
    )
    grad_w = lax.psum(weight_part, ("ew", "ns")).astype(jnp.bfloat16)
    return (grad_tokens, grad_w)


def solution(mesh):
    in_specs = (P("ns", "ew", None), P(), P("ns", "ew", None))
    out_specs = (P("ns", "ew", None), P())
    return jax.shard_map(local, mesh=mesh, in_specs=in_specs, out_specs=out_specs, check_vma=False)
```
